256 devices in a mesh: pool: 32 (over z, x), tp: 8 (over y, core).
Axes of the slice: x: 4, y: 4, z: 8, core: 2. Of those that a mesh axis runs over, the one named last changes fastest.
Arguments:
- hidden_rows: bfloat16 [1024, 8192], P('pool', 'tp'), may hold values from -6 to 6
- queries: bfloat16 [1024, 8192], P('pool', 'tp'), may hold values from -48 to 48
- w_kv: bfloat16 [8192, 2, 1024], P(None, None, 'tp'), may hold values from -0.0625 to 0.0625
- adapters_down: bfloat16 [512, 8192, 128], P('pool', 'tp'), may hold values from -0.0625 to 0.0625
- adapters_up: bfloat16 [512, 2, 64, 1024], P('pool', None, None, 'tp'), may hold values from -0.75 to 0.75
- kv_pages: bfloat16 [256, 128, 2, 1024], P('pool', None, None, 'tp'), may hold values from -48 to 48
- tenant_ids: int32 [1024], P('pool'), may hold values from 0 to 511, as said below
- owner_table: int32 [512], replicated, may hold values from 0 to 511, as said below
- page_tables: int32 [1024, 16], P('pool'), may hold values from 0 to 7
- lengths: int32 [1024], P('pool'), may hold values from 1 to 2048, as said below
Outputs:
- attention: bfloat16 [1024, 8192], P('pool', 'tp')
- new_kv: bfloat16 [1024, 2, 1024], P('pool', None, 'tp')
The draws below stay inside these ranges and needn't reach their ends.
Inputs may be any that keep to these rules, and one draw needn't show every extreme that they name: A permutation: each storage row holds one tenant's adapter; the owner of tenant t is owner_table[t] // 16. `tenant_ids`: among the 32 blocks of one index of pool, at most 2 name tenants whose adapters have the same owner, and on every index some owner has exactly 2 of them. `lengths`: on every index of pool some row has 2048.
All inputs are finite; a program needn't handle non-finite values.
Results may differ from the reference program's by a relative error of at most 0.012.
Values may be sent and summed in bfloat16 or wider, within the bound.
No kernel may reach another device: no remote copies, remote signals or barrier semaphores. Data moves between devices by JAX's collectives and lax.ppermute only.
A program may use at most 128 MiB of HBM per device.

```python
import math
import jax
import jax.numpy as jnp
from jax import lax

D = 8192
HEADS = 64
KV_HEADS = 8
HD = 128
ADAPTER_RANK = 64
POOL_ROWS = 32
TENANT_BLOCKS = 32
ADP_DEV = 16
PAGES_DEV = 8
PAGE = 128
MAXP = 16
ROWS = 1024
BLOCKS_ALL = 1024
MOST = 2
ADAPTERS = 512
PAGES_ALL = 256
CTX = 2048
KEY_VALUE_WIDTH = 1024
QD = 8192
N_POOL = 32


def tenant_layout(key):
    adapter_table = jax.random.permutation(jax.random.fold_in(key, 101), ADAPTERS).astype(jnp.int32)
    inverse = jnp.argsort(adapter_table, stable=True).astype(jnp.int32)

    def one_replica(replica_key):
        owner_key, place_key, slot_key = jax.random.split(replica_key, 3)
        owners = jax.random.permutation(owner_key, N_POOL).astype(jnp.int32)
        places = jax.random.permutation(place_key, TENANT_BLOCKS).astype(jnp.int32)
        others = owners[1 + jnp.maximum(places - MOST, 0) % (N_POOL - 1)]
        chosen = jnp.where(places < MOST, owners[0], others)
        slot_draw = jax.random.randint(slot_key, (TENANT_BLOCKS,), 0, ADP_DEV).astype(jnp.int32)
        return inverse[chosen * ADP_DEV + slot_draw]
    replica_keys = jax.random.split(jax.random.fold_in(key, 202), N_POOL)
    tenants = jax.vmap(one_replica)(replica_keys).reshape(-1).astype(jnp.int32)
    return (adapter_table, tenants)


def draw_owner_table(key, part):
    adapter_table, tenants = tenant_layout(key)
    return adapter_table


def draw_tenant_ids(key, part):
    adapter_table, tenants = tenant_layout(key)
    return tenants


def draw_lengths(key, part):
    key = jax.random.fold_in(key, 3)
    length_key, pick_key = jax.random.split(key)
    drawn = jax.random.randint(length_key, (ROWS,), 1, CTX + 1).astype(jnp.int32)
    longest = jax.random.randint(pick_key, (N_POOL,), 0, POOL_ROWS).astype(jnp.int32) + jnp.arange(N_POOL, dtype=jnp.int32) * POOL_ROWS
    return drawn.at[longest].set(CTX)


def draw_queries(key, part):
    key = jax.random.fold_in(key, 5)
    normal_key = jax.random.fold_in(key, 0)
    drawn = jax.random.normal(normal_key, (ROWS, HEADS, HD), jnp.float32)
    return drawn.reshape(ROWS, QD).astype(jnp.bfloat16)


def draw_kv_pages(key, part):
    key = jax.random.fold_in(key, 7)
    drawn = jax.random.normal(key, (PAGES_ALL, PAGE, 2, KV_HEADS, HD), jnp.float32)
    return drawn.reshape(PAGES_ALL, PAGE, 2, KEY_VALUE_WIDTH).astype(jnp.bfloat16)


def with_ends(entries, own_key, low, high):
    dims = entries.shape
    spot = [jax.random.randint(jax.random.fold_in(own_key, axis), (), 0, dims[axis]) for axis in range(len(dims))]
    entries = entries.at[tuple(spot)].set(low)
    longest = dims.index(max(dims))
    spot[longest] = (spot[longest] + 1) % dims[longest]
    return entries.at[tuple(spot)].set(high)


def level_of(stream_key, dims, cuts, low, high):
    def one(dim, blocks):
        draws = jax.random.uniform(jax.random.fold_in(jax.random.fold_in(stream_key, 6), dim), (blocks,), jnp.float32, low / len(cuts), high / len(cuts))
        return jnp.repeat(jnp.exp(draws), dims[dim] // blocks).reshape((-1,) + (1,) * (len(dims) - dim - 1))

    loudness = one(*cuts[0])
    for cut in cuts[1:]:
        loudness = loudness * one(*cut)
    return loudness


def gaussian(stream_key, extent, scale, reach, shards=(), kind=jnp.bfloat16):
    loudness = level_of(stream_key, extent, shards, -0.22, 0.18) if shards else 1.0
    entries = jax.random.normal(stream_key, extent, jnp.float32) * scale * loudness
    return jnp.minimum(jnp.maximum(entries, -reach), reach).astype(kind)


def setup_inputs(seed: int = 0) -> dict:
    key_list = jax.random.split(jax.random.key(seed), 11)
    hidden_rows = gaussian(key_list[0], (ROWS, D), 1.0, 6.0, ((0, 32), (1, 8)))
    queries = draw_queries(jax.random.fold_in(key_list[10], 71), 0)
    w_kv = gaussian(key_list[2], (D, 2, KEY_VALUE_WIDTH), D ** -0.5, 0.0625, ((2, 8),))
    adapters_down = gaussian(key_list[3], (ADAPTERS, D, 2 * ADAPTER_RANK), D ** -0.5, 0.0625, ((0, 32), (1, 8)))
    adapters_up = gaussian(key_list[4], (ADAPTERS, 2, ADAPTER_RANK, KEY_VALUE_WIDTH), ADAPTER_RANK ** -0.5, 0.75, ((0, 32), (3, 8)))
    kv_pages = draw_kv_pages(jax.random.fold_in(key_list[10], 71), 0)
    tenant_ids = draw_tenant_ids(jax.random.fold_in(key_list[10], 71), 0)
    owner_table = draw_owner_table(jax.random.fold_in(key_list[10], 71), 0)
    page_tables = with_ends(jax.random.randint(key_list[8], (BLOCKS_ALL, MAXP), 0, PAGES_DEV), jax.random.fold_in(key_list[8], 1), 0, PAGES_DEV - 1).astype(jnp.int32)
    lengths = draw_lengths(jax.random.fold_in(key_list[10], 71), 0)
    return {"hidden_rows": hidden_rows, "queries": queries, "w_kv": w_kv, "adapters_down": adapters_down, "adapters_up": adapters_up, "kv_pages": kv_pages, "tenant_ids": tenant_ids, "owner_table": owner_table, "page_tables": page_tables, "lengths": lengths}


adapter_scale = 0.5

def rotate(key_heads, positions):
    half_dim = key_heads.shape[-1] // 2
    frequency = 10000.0 ** (-jnp.arange(half_dim, dtype=jnp.float32) * 2.0 / key_heads.shape[-1])
    angles = positions.astype(jnp.float32)[:, None, None] * frequency
    cosine = jnp.cos(angles)
    sine_part = jnp.sin(angles)
    lower_half = key_heads[..., :half_dim]
    upper_half = key_heads[..., half_dim:]
    return jnp.concatenate([lower_half * cosine - upper_half * sine_part, upper_half * cosine + lower_half * sine_part], -1)

def attend(query_blocks, key_pages, value_pages, key_new, value_new, block_lengths):
    score_scale = 1.0 / math.sqrt(HD)
    scores = jnp.einsum('bkghd,btgd->bkght', query_blocks.astype(jnp.float32), key_pages.astype(jnp.float32)) * score_scale
    live_mask = jnp.arange(key_pages.shape[1], dtype=jnp.int32)[None, None, :] < block_lengths[:, :, None]
    scores = jnp.where(live_mask[:, :, None, None, :], scores, -jnp.inf)
    own_score = jnp.einsum('bkghd,bkgd->bkgh', query_blocks.astype(jnp.float32), key_new.astype(jnp.float32)) * score_scale
    row_top = jnp.maximum(lax.optimization_barrier(jnp.max(scores, -1)), own_score)
    weights = jnp.exp(scores - row_top[..., None])
    own_weight = jnp.exp(own_score - row_top)
    totals = lax.optimization_barrier(jnp.sum(weights, -1)) + own_weight
    prob_rows = (weights / totals[..., None]).astype(jnp.bfloat16)
    own_prob = (own_weight / totals).astype(jnp.bfloat16)
    mixture = jnp.einsum('bkght,btgd->bkghd', prob_rows.astype(jnp.float32), value_pages.astype(jnp.float32))
    mixture = mixture + own_prob.astype(jnp.float32)[..., None] * value_new.astype(jnp.float32)[:, :, :, None, :]
    return mixture.astype(jnp.bfloat16)

def reference(hidden_rows, queries, w_kv, adapters_down, adapters_up, kv_pages, tenant_ids, owner_table, page_tables, lengths):
    storage = owner_table[tenant_ids]
    rows_per_block = POOL_ROWS // TENANT_BLOCKS
    group_size = HEADS // KV_HEADS

    def replica(index):
        row_start = index * POOL_ROWS
        rows_here = lax.dynamic_slice_in_dim(hidden_rows, row_start, POOL_ROWS, 0)
        query_here = lax.dynamic_slice_in_dim(queries, row_start, POOL_ROWS, 0)
        length_here = lax.dynamic_slice_in_dim(lengths, row_start, POOL_ROWS, 0)
        slots_here = lax.dynamic_slice_in_dim(storage, index * TENANT_BLOCKS, TENANT_BLOCKS, 0)
        tables_here = lax.dynamic_slice_in_dim(page_tables, index * TENANT_BLOCKS, TENANT_BLOCKS, 0)
        pages_here = lax.dynamic_slice_in_dim(kv_pages, index * PAGES_DEV, PAGES_DEV, 0)
        base_key_value = jnp.dot(rows_here, w_kv.reshape(D, 2 * KEY_VALUE_WIDTH), preferred_element_type=jnp.float32).reshape(POOL_ROWS, 2, KEY_VALUE_WIDTH)
        down_weight_blocks = adapters_down[slots_here]
        up_weight_blocks = adapters_up[slots_here]
        input_blocks = rows_here.reshape(TENANT_BLOCKS, rows_per_block, D)
        reduced_rank_rows = jnp.einsum('hpm,hmi->hpi', input_blocks.astype(jnp.float32), down_weight_blocks.astype(jnp.float32)).astype(jnp.bfloat16)
        adapter_term = jnp.einsum('ztpa,zpan->ztpn', reduced_rank_rows.reshape(TENANT_BLOCKS, rows_per_block, 2, ADAPTER_RANK).astype(jnp.float32), up_weight_blocks.astype(jnp.float32))
        combined_output = base_key_value + adapter_scale * adapter_term.reshape(POOL_ROWS, 2, KEY_VALUE_WIDTH)
        key_new = rotate(combined_output[:, 0].reshape(POOL_ROWS, KV_HEADS, HD), length_here).reshape(POOL_ROWS, KEY_VALUE_WIDTH)
        new_kv = jnp.stack([key_new, combined_output[:, 1]], 1).astype(jnp.bfloat16)
        gathered = pages_here[tables_here]
        key_pages = gathered[:, :, :, 0].reshape(TENANT_BLOCKS, CTX, KV_HEADS, HD)
        value_pages = gathered[:, :, :, 1].reshape(TENANT_BLOCKS, CTX, KV_HEADS, HD)
        query_blocks = query_here.reshape(TENANT_BLOCKS, rows_per_block, KV_HEADS, group_size, HD)
        new_blocks = new_kv.reshape(TENANT_BLOCKS, rows_per_block, 2, KV_HEADS, HD)
        mixture = attend(query_blocks, key_pages, value_pages, new_blocks[:, :, 0], new_blocks[:, :, 1], length_here.reshape(TENANT_BLOCKS, rows_per_block))
        return (mixture.reshape(POOL_ROWS, QD), new_kv)
    attention, new_kv = lax.map(replica, jnp.arange(N_POOL, dtype=jnp.int32))
    return (attention.reshape(ROWS, QD), new_kv.reshape(ROWS, 2, KEY_VALUE_WIDTH))
```

```python
import math

import jax
import jax.numpy as jnp
from jax import lax
from jax.experimental import pallas as pl
from jax.experimental.pallas import tpu as pltpu
from jax.sharding import PartitionSpec as P

HD = 128
ADAPTER_SCALE = 0.5
BF = jnp.bfloat16
F32 = jnp.float32
I32 = jnp.int32
VMEM = pl.BlockSpec(memory_space=pltpu.VMEM)
SMEM = pl.BlockSpec(memory_space=pltpu.SMEM)


def iota(shape, dim):
    return lax.broadcasted_iota(I32, shape, dim)


def mm(a, b):
    return jnp.dot(a, b, preferred_element_type=F32)


def mm_t(a, b):
    return lax.dot_general(a, b, (((1,), (1,)), ((), ())), preferred_element_type=F32)


def onehot(mask):
    return jnp.where(mask, 1.0, 0.0).astype(BF)


def column(row, n):
    return jnp.sum(jnp.where(iota((n, n), 0) == iota((n, n), 1), row, 0.0), 1, keepdims=True)


def chunked(x):
    return jnp.concatenate([x[:, i * HD : (i + 1) * HD] for i in range(x.shape[1] // HD)], 0)


def call(body, outs, n_in, flops=0, read=0, scratch=(), limit=16, smem=()):
    return pl.pallas_call(
        body,
        out_shape=outs,
        in_specs=[SMEM if i in smem else VMEM for i in range(n_in)],
        out_specs=jax.tree.map(lambda _: VMEM, outs),
        scratch_shapes=scratch,
        compiler_params=pltpu.CompilerParams(vmem_limit_bytes=limit << 20),
        cost_estimate=pl.CostEstimate(flops=flops, bytes_accessed=read, transcendentals=0),
    )


def route_body(hidden_ref, tenants_ref, table_ref, send_ref, dest_ref):
    n = tenants_ref.shape[1]
    tenant = column(tenants_ref[...].astype(F32), n)
    entries = table_ref.shape[1]
    table = table_ref[...].astype(F32)
    lanes = iota((n, entries), 1).astype(F32)
    storage = jnp.sum(jnp.where(tenant == lanes, table, 0.0), 1, keepdims=True).astype(I32)
    owner = storage >> 4
    slot = storage & 15
    eye = iota((n, n), 0) == iota((n, n), 1)
    owner_row = jnp.sum(jnp.where(eye, owner.astype(F32), 0.0), 0, keepdims=True)
    same = (owner.astype(F32) == owner_row) & (iota((n, n), 1) < iota((n, n), 0))
    rank = jnp.sum(jnp.where(same, 1.0, 0.0), 1, keepdims=True)
    dest = owner.astype(F32) * 2.0 + rank
    dest_ref[...] = jnp.broadcast_to(dest, dest_ref.shape)
    wide = (iota((n, 8 * n), 1) & (n - 1)) == iota((n, 8 * n), 0)
    dest_wide = jnp.sum(jnp.where(wide, dest, 0.0), 0, keepdims=True).astype(I32)
    slot_row = jnp.sum(jnp.where(eye, slot.astype(F32), 0.0), 0, keepdims=True)
    dest_row = jnp.sum(jnp.where(eye, dest, 0.0), 0, keepdims=True).astype(I32)
    i = iota((16 * n, 8 * n), 0)
    pick = onehot(((i >> 3) == dest_wide) & ((i & 7) == (iota((16 * n, 8 * n), 1) >> 5)))
    send_ref[:, 0:16, :] = mm(pick, chunked(hidden_ref[...])).astype(BF).reshape(n, 16, HD)
    i = iota((8 * n, n), 0)
    slots = jnp.where((i >> 3) * 2 + (i & 1) == dest_row, slot_row, 0.0)
    slots = jnp.sum(slots, 1, keepdims=True)
    send_ref[:, 16:24, :] = (
        jnp.broadcast_to(slots, (8 * n, HD)).astype(BF).reshape(n, 8, HD)
    )


def down_body(recv_ref, down_ref, part_ref, slot_ref):
    n = recv_ref.shape[0]
    m = 2 * n
    rows = recv_ref[:, 0:16, :].reshape(16 * n, HD)
    i, j = iota((16 * n, 16 * n), 0), iota((16 * n, 16 * n), 1)
    order = onehot((i >> 6) + (i & (m - 1)) * 8 == j)
    x = mm(order, rows).astype(BF)
    x = jnp.concatenate([x[c * m : (c + 1) * m] for c in range(8)], 1)
    i, j = iota((m, 8 * n), 0), iota((m, 8 * n), 1)
    slot = mm(onehot((i >> 1) * 8 + (i & 1) == j), recv_ref[:, 16:24, :].reshape(8 * n, HD))
    slot_ref[...] = slot
    total = jnp.zeros((m, HD), F32)
    for a in range(0, down_ref.shape[0], 2):
        y = mm(x, jnp.concatenate([down_ref[a], down_ref[a + 1]], 1))
        total = total + jnp.where(slot == a, y[:, :HD], 0.0)
        total = total + jnp.where(slot == a + 1, y[:, HD:], 0.0)
    part_ref[...] = total


def up_body(p0_ref, p1_ref, p2_ref, p3_ref, slot_ref, up_ref, send_ref):
    m = slot_ref.shape[0]
    n = m // 2
    down = (p0_ref[...] + p1_ref[...]) + (p2_ref[...] + p3_ref[...])
    first = iota((m, HD), 1) < HD // 2
    both = jnp.concatenate([jnp.where(first, down, 0.0), jnp.where(first, 0.0, down)], 0)
    slot = jnp.concatenate([slot_ref[...]] * 2, 0)
    count = up_ref.shape[0] // HD
    picked = jnp.concatenate(
        [jnp.where(slot == a, both, 0.0).astype(BF) for a in range(count)], 1
    )
    lora = mm(picked, up_ref[...])
    high = lora.astype(BF)
    low = (lora - high.astype(F32)).astype(BF)
    i, j = iota((8 * n, 4 * m), 0), iota((8 * n, 4 * m), 1)
    q = i & 7
    want = (q >> 2) * (2 * m) + (q & 1) * m + (i >> 3) * 2 + ((q >> 1) & 1)
    send = mm(onehot(want == j), jnp.concatenate([high, low], 0))
    send_ref[...] = send.astype(BF).reshape(n, 8, HD)


def base_body(index_ref, x0_ref, x1_ref, y1_ref, y2_ref, y3_ref, w_ref, out_ref):
    me = index_ref[0]
    n = x0_ref.shape[0]
    width = x0_ref.shape[1]
    chunks = width // HD
    i, j = iota((HD, 4 * HD), 0), iota((HD, 4 * HD), 1)
    spread = onehot((j & 255) == 2 * i + (j >> 8))
    total = jnp.zeros((2 * n, HD), F32)
    for dy in range(4):
        for dc in range(2):
            if dy == 0:
                x = (x0_ref, x1_ref)[dc][...]
            else:
                x = (y1_ref, y2_ref, y3_ref)[dy - 1][dc]
            peer = (((me >> 1) + 4 - dy) & 3) * 2 + ((me & 1) ^ dc)
            e = mm(chunked(x), spread).astype(BF)
            both = jnp.concatenate(
                [
                    jnp.concatenate(
                        [e[g * n : (g + 1) * n, c * 256 : (c + 1) * 256] for g in range(chunks)], 1
                    )
                    for c in range(2)
                ],
                0,
            )
            at = pl.multiple_of(peer * (2 * width), 2 * width)
            total = total + mm(both, w_ref[pl.ds(at, 2 * width), :])
    out_ref[...] = total


def cached_body(q_ref, pages_ref, tables_ref, lengths_ref, mix_ref, top_ref, sum_ref):
    n = q_ref.shape[0]
    heads = q_ref.shape[1] // HD
    page = HD
    count = pages_ref.shape[0] // (2 * page)
    tokens = count * page
    eye = onehot(iota((n, n), 0) == iota((n, n), 1))
    tables = mm_t(eye, tables_ref[...].astype(F32).astype(BF)).astype(I32)
    length = column(lengths_ref[...].astype(F32), n).astype(I32)
    at = iota((n, tokens), 1)
    page_id, place = at >> 7, at & (page - 1)
    counts = jnp.zeros((n, tokens), F32)
    for j in range(tables_ref.shape[0]):
        hit = (tables[:, j : j + 1] == page_id) & (place < length - j * page)
        counts = counts + jnp.where(hit, 1.0, 0.0)
    i, j = iota((2 * page, 2 * page), 0), iota((2 * page, 2 * page), 1)
    part = onehot((i & (page - 1)) * 2 + (i >> 7) == j)
    keys, values = [], []
    for p in range(count):
        both = mm(part, pages_ref[p * 2 * page : (p + 1) * 2 * page, :]).astype(BF)
        keys.append(both[:page])
        values.append(both[page:])
    keys = jnp.concatenate(keys, 0)
    values = jnp.concatenate(values, 0)
    for h in range(heads):
        scores = mm_t(q_ref[:, h * HD : (h + 1) * HD], keys) * (1.0 / math.sqrt(HD))
        scores = jnp.where(counts > 0.0, scores, -jnp.inf)
        top = jnp.max(scores, 1, keepdims=True)
        weights = jnp.exp(scores - top) * counts
        rows = slice(h * n, (h + 1) * n)
        mix_ref[rows, :] = mm(weights.astype(BF), values)
        top_ref[rows, :] = jnp.broadcast_to(top, (n, HD))
        sum_ref[rows, :] = jnp.broadcast_to(jnp.sum(weights, 1, keepdims=True), (n, HD))


def finish_body(
    recv_ref, dest_ref, base_ref, cos_ref, sin_ref, q_ref, mix_ref, top_ref, sum_ref, att_ref, new_ref
):
    n = recv_ref.shape[0]
    heads = q_ref.shape[1] // HD
    dest = dest_ref[...].astype(I32)
    dest = jnp.concatenate([dest, dest], 1)
    dest = jnp.concatenate([dest, dest], 0)
    i, j = iota((2 * n, 8 * n), 0), iota((2 * n, 8 * n), 1)
    back = onehot((dest == (j >> 3) * 2 + ((j >> 1) & 1)) & ((j & 1) == (i >> 5)))
    lora = mm(back, recv_ref[...].reshape(8 * n, HD))
    combined = base_ref[...] + ADAPTER_SCALE * lora
    key = combined[:n]
    half = HD // 2
    turned = jnp.concatenate([key[:, half:], key[:, :half]], 1)
    key = key * cos_ref[...] + turned * sin_ref[...]
    new = jnp.concatenate([key, combined[n:]], 0).astype(BF)
    i, j = iota((2 * n, 2 * n), 0), iota((2 * n, 2 * n), 1)
    new_ref[...] = mm(onehot((i & 1) * n + (i >> 1) == j), new).astype(BF)
    key = new[:n].astype(F32)
    value = new[n:].astype(F32)
    for h in range(heads):
        rows = slice(h * n, (h + 1) * n)
        q = q_ref[:, h * HD : (h + 1) * HD].astype(F32)
        own = jnp.sum(q * key, 1, keepdims=True) * (1.0 / math.sqrt(HD))
        top = top_ref[rows, :]
        high = jnp.maximum(top, own)
        old = jnp.exp(top - high)
        mine = jnp.exp(own - high)
        mixed = mix_ref[rows, :] * old + mine * value
        att_ref[:, h * HD : (h + 1) * HD] = (mixed / (sum_ref[rows, :] * old + mine)).astype(BF)


def shape(dims, dtype):
    return jax.ShapeDtypeStruct(dims, dtype)


def per_device(
    hidden, queries, w_kv, adapters_down, adapters_up, kv_pages, tenant_ids, owner_table, page_tables, lengths
):
    n = hidden.shape[0]
    width = hidden.shape[1]

    def swap_core(a):
        return lax.ppermute(a, "tp", [(i, i ^ 1) for i in range(8)])

    def along_y(a):
        return [
            lax.ppermute(a, "tp", [(i, ((i // 2 + d) % 4) * 2 + i % 2) for i in range(8)])
            for d in (1, 2, 3)
        ]

    send, dest = call(
        route_body, (shape((n, 24, HD), BF), shape((n, HD), F32)), 3, 2 * 512 * 256 * 128, 300000
    )(hidden, tenant_ids.reshape(1, -1), owner_table.reshape(1, -1))
    recv = lax.all_to_all(send, "pool", 0, 0, tiled=True)

    other = swap_core(hidden)
    pair = jnp.stack([hidden, other])
    far = along_y(pair)
    half = HD // 2
    frequency = 10000.0 ** (-jnp.arange(half, dtype=F32) * 2.0 / HD)
    angles = lengths.astype(F32)[:, None] * frequency
    cosine, sine = jnp.cos(angles), jnp.sin(angles)
    cosine = jnp.concatenate([cosine, cosine], 1)
    sine = jnp.concatenate([-sine, sine], 1)
    pages = kv_pages.reshape(-1, HD)
    group = shape((8 * n, HD), F32)
    mix, top, total = call(cached_body, (group, group, group), 4, 4 * 256 * 1024 * 128, 10000000)(
        queries, pages, page_tables.T, lengths.reshape(1, -1)
    )
    me = lax.axis_index("tp").astype(I32).reshape(1)
    base = call(base_body, shape((2 * n, HD), F32), 7, 4 * 64 * 8192 * 128, 8000000, smem=(0,))(
        me, hidden, other, *far, w_kv.reshape(-1, HD)
    )

    part, slot = call(
        down_body, (shape((2 * n, HD), F32), shape((2 * n, HD), F32)), 2, 2 * 64 * 16 * 1024 * 128, 4500000
    )(recv, adapters_down)
    part = part + swap_core(part)
    sums = along_y(part)
    back = call(up_body, shape((n, 8, HD), BF), 6, 2 * 128 * 2048 * 128, 600000)(
        part, *sums, slot, adapters_up.reshape(-1, HD)
    )
    back = lax.all_to_all(back, "pool", 0, 0, tiled=True)

    attention, new_kv = call(
        finish_body, (shape((n, width), BF), shape((2 * n, HD), BF)), 9, 1000000, 1000000
    )(back, dest, base, cosine, sine, queries, mix, top, total)
    return attention, new_kv.reshape(n, 2, HD)


def solution(mesh):
    in_specs = (
        P("pool", "tp"),
        P("pool", "tp"),
        P(None, None, "tp"),
        P("pool", "tp", None),
        P("pool", None, None, "tp"),
        P("pool", None, None, "tp"),
        P("pool"),
        P(),
        P("pool", None),
        P("pool"),
    )
    out_specs = (P("pool", "tp"), P("pool", None, "tp"))
    return jax.shard_map(
        per_device, mesh=mesh, in_specs=in_specs, out_specs=out_specs, check_vma=False
    )
```

```python
import math

import jax
import jax.numpy as jnp
from jax import lax
from jax.experimental import pallas as pl
from jax.experimental.pallas import tpu as pltpu
from jax.sharding import PartitionSpec as P

HD = 128
ADAPTER_SCALE = 0.5
BF = jnp.bfloat16
F32 = jnp.float32
I32 = jnp.int32
VMEM = pl.BlockSpec(memory_space=pltpu.VMEM)
SMEM = pl.BlockSpec(memory_space=pltpu.SMEM)
HBM = pl.BlockSpec(memory_space=pl.ANY)
ALL = 58
MOST = 52
CHUNK = 18


def iota(shape, dim):
    return lax.broadcasted_iota(I32, shape, dim)


def mm(a, b):
    return jnp.dot(a, b, preferred_element_type=F32)


def mm_t(a, b):
    return lax.dot_general(a, b, (((1,), (1,)), ((), ())), preferred_element_type=F32)


def onehot(mask):
    return jnp.where(mask, 1.0, 0.0).astype(BF)


def column(row, n):
    return jnp.sum(jnp.where(iota((n, n), 0) == iota((n, n), 1), row, 0.0), 1, keepdims=True)


def chunked(x):
    return jnp.concatenate([x[:, i * HD : (i + 1) * HD] for i in range(x.shape[1] // HD)], 0)


def call(body, outs, n_in, flops=0, read=0, scratch=(), limit=16, smem=(), far=()):
    return pl.pallas_call(
        body,
        out_shape=outs,
        in_specs=[SMEM if i in smem else HBM if i in far else VMEM for i in range(n_in)],
        out_specs=jax.tree.map(lambda _: VMEM, outs),
        scratch_shapes=scratch,
        compiler_params=pltpu.CompilerParams(vmem_limit_bytes=limit << 20),
        cost_estimate=pl.CostEstimate(flops=flops, bytes_accessed=read, transcendentals=0),
    )


def fetch(sources, targets, sems):
    copies = [
        pltpu.make_async_copy(source, target, sems.at[i])
        for i, (source, target) in enumerate(zip(sources, targets))
    ]
    for copy in copies:
        copy.start()
    return copies


def route_body(
    hidden_at, tenants_at, table_at, send_ref, dest_ref, own_ref, hidden_ref, tenants_ref, table_ref, sems
):
    copies = fetch(
        (tenants_at, table_at, hidden_at), (tenants_ref, table_ref, hidden_ref), sems
    )
    copies[0].wait()
    copies[1].wait()
    n = tenants_ref.shape[1]
    tenant = column(tenants_ref[...].astype(F32), n)
    entries = table_ref.shape[1]
    table = table_ref[...].astype(F32)
    lanes = iota((n, entries), 1).astype(F32)
    storage = jnp.sum(jnp.where(tenant == lanes, table, 0.0), 1, keepdims=True).astype(I32)
    owner = (storage >> 4).astype(F32)
    slot = (storage & 15).astype(F32)
    eye = iota((n, n), 0) == iota((n, n), 1)
    owner_row = jnp.sum(jnp.where(eye, owner, 0.0), 0, keepdims=True)
    same = (owner == owner_row) & (iota((n, n), 1) < iota((n, n), 0))
    rank = jnp.sum(jnp.where(same, 1.0, 0.0), 1, keepdims=True)
    dest = owner * 2.0 + rank
    dest_ref[...] = jnp.broadcast_to(dest, dest_ref.shape)
    wide = (iota((n, 8 * n), 1) & (n - 1)) == iota((n, 8 * n), 0)
    dest_wide = jnp.sum(jnp.where(wide, dest, 0.0), 0, keepdims=True).astype(I32)
    dest_row = dest_wide[:, :n]
    i = iota((CHUNK * n, 1), 0)
    chunk = (i * 3641) >> 16
    rest = i - CHUNK * chunk
    place, part = chunk * 2 + (rest & 1), rest >> 1
    where_from = iota((1, 8 * n), 1)
    pick = onehot((place == dest_wide) & (part == (where_from >> 5)))
    pick_slot = onehot((place == dest_row) & (part == 8))
    slots = jnp.broadcast_to(slot, (n, HD)).astype(BF)
    sent = mm(pick_slot, slots)
    copies[2].wait()
    send_ref[...] = (sent + mm(pick, chunked(hidden_ref[...]))).astype(BF)
    own_ref[...] = hidden_ref[...]


def down_body(*refs):
    recv_ref, down_at = refs[:2]
    part_ref, slot_ref, down_ref, sems = refs[-4:]
    count = down_ref.shape[0]
    parts = sems.shape[0]
    each = count // parts
    pieces = [slice(k * each, (k + 1) * each) for k in range(parts)]
    copies = fetch([down_at.at[p] for p in pieces], [down_ref.at[p] for p in pieces], sems)
    n = recv_ref.shape[0] // CHUNK
    m = 2 * n
    rows = recv_ref[...]
    i, j = iota((8 * m, 1), 0), iota((1, CHUNK * n), 1)
    order = onehot(((i & (m - 1)) >> 1) * CHUNK + (i >> 6) * 2 + (i & 1) == j)
    x = mm(order, rows).astype(BF)
    x = jnp.concatenate([x[c * m : (c + 1) * m] for c in range(8)], 1)
    i = iota((m, 1), 0)
    slot = mm(onehot((i >> 1) * CHUNK + 16 + (i & 1) == j), rows)
    slot_ref[...] = slot
    total = jnp.zeros((m, HD), F32)
    for a in range(0, count, 2):
        if a % each == 0:
            copies[a // each].wait()
        y = mm(x, jnp.concatenate([down_ref[a], down_ref[a + 1]], 1))
        total = total + jnp.where(slot == a, y[:, :HD], 0.0)
        total = total + jnp.where(slot == a + 1, y[:, HD:], 0.0)
    part_ref[...] = total


def up_body(p0_ref, p1_ref, p2_ref, p3_ref, slot_ref, up_ref, send_ref):
    m = slot_ref.shape[0]
    down = (p0_ref[...] + p1_ref[...]) + (p2_ref[...] + p3_ref[...])
    first = iota((m, HD), 1) < HD // 2
    both = jnp.concatenate([jnp.where(first, down, 0.0), jnp.where(first, 0.0, down)], 0)
    slot = jnp.concatenate([slot_ref[...]] * 2, 0)
    count = up_ref.shape[0] // HD
    picked = jnp.concatenate(
        [jnp.where(slot == a, both, 0.0).astype(BF) for a in range(count)], 1
    )
    lora = mm(picked, up_ref[...])
    i, j = iota((2 * m, 1), 0), iota((1, 2 * m), 1)
    order = onehot((i & 1) * m + (i >> 1) == j)
    send_ref[...] = mm(order, lora.astype(BF)).astype(BF)


def base_body(index_ref, x0_ref, x1_ref, y1_ref, y2_ref, y3_ref, w_at, out_ref, w_ref, sems):
    me = index_ref[0]
    n = x0_ref.shape[0]
    width = x0_ref.shape[1]
    away = [(dy, dc) for dy in range(4) for dc in range(2)]
    spots = []
    for dy, dc in away:
        peer = (((me >> 1) + 4 - dy) & 3) * 2 + ((me & 1) ^ dc)
        spots.append(pl.ds(pl.multiple_of(peer * (2 * width), 2 * width), 2 * width))
    copies = fetch([w_at.at[p] for p in spots], [w_ref.at[k] for k in range(8)], sems)
    chunks = width // HD
    i, j = iota((HD, 4 * HD), 0), iota((HD, 4 * HD), 1)
    spread = onehot((j & 255) == 2 * i + (j >> 8))
    total = jnp.zeros((2 * n, HD), F32)
    for k, (dy, dc) in enumerate(away):
        if dy == 0:
            x = (x0_ref, x1_ref)[dc][...]
        else:
            x = (y1_ref, y2_ref, y3_ref)[dy - 1][dc]
        e = mm(chunked(x), spread).astype(BF)
        both = jnp.concatenate(
            [
                jnp.concatenate(
                    [e[g * n : (g + 1) * n, c * 256 : (c + 1) * 256] for g in range(chunks)], 1
                )
                for c in range(2)
            ],
            0,
        )
        copies[k].wait()
        total = total + mm(both, w_ref[k])
    out_ref[...] = total


def cached_body(
    q_at, pages_at, tables_at, lengths_at, cache_ref, q_ref, pages_ref, tables_ref, lengths_ref, sems
):
    copies = fetch(
        (tables_at, lengths_at, q_at, pages_at), (tables_ref, lengths_ref, q_ref, pages_ref), sems
    )
    copies[0].wait()
    copies[1].wait()
    n = q_ref.shape[0]
    heads = q_ref.shape[1] // HD
    page = HD
    count = pages_ref.shape[0] // (2 * page)
    tokens = count * page
    eye = onehot(iota((n, n), 0) == iota((n, n), 1))
    tables = mm_t(eye, tables_ref[...].astype(F32).astype(BF)).astype(I32)
    length = column(lengths_ref[...].astype(F32), n).astype(I32)
    at = iota((n, tokens), 1)
    page_id, place = at >> 7, at & (page - 1)
    counts = jnp.zeros((n, tokens), F32)
    for j in range(tables_ref.shape[0]):
        hit = (tables[:, j : j + 1] == page_id) & (place < length - j * page)
        counts = counts + jnp.where(hit, 1.0, 0.0)
    i, j = iota((2 * page, 2 * page), 0), iota((2 * page, 2 * page), 1)
    part = onehot((i & (page - 1)) * 2 + (i >> 7) == j)
    copies[2].wait()
    copies[3].wait()
    keys, values = [], []
    for p in range(count):
        both = mm(part, pages_ref[p * 2 * page : (p + 1) * 2 * page, :]).astype(BF)
        keys.append(both[:page])
        values.append(both[page:])
    keys = jnp.concatenate(keys, 0)
    values = jnp.concatenate(values, 0)
    for h in range(heads):
        scores = mm_t(q_ref[:, h * HD : (h + 1) * HD], keys) * (1.0 / math.sqrt(HD))
        scores = jnp.where(counts > 0.0, scores, -jnp.inf)
        top = jnp.max(scores, 1, keepdims=True)
        weights = jnp.exp(scores - top) * counts
        rows = slice(h * n, (h + 1) * n)
        cache_ref[0, rows, :] = mm(weights.astype(BF), values)
        cache_ref[1, rows, :] = jnp.broadcast_to(top, (n, HD))
        cache_ref[2, rows, :] = jnp.broadcast_to(jnp.sum(weights, 1, keepdims=True), (n, HD))


def finish_body(
    recv_ref, dest_ref, base_ref, cos_ref, sin_ref, q_ref, cache_ref, att_ref, new_ref
):
    n = q_ref.shape[0]
    heads = q_ref.shape[1] // HD
    dest = dest_ref[...].astype(I32)
    dest = jnp.concatenate([dest, dest], 0)
    i, j = iota((2 * n, 1), 0), iota((1, 4 * n), 1)
    back = onehot((dest == (j >> 1)) & ((j & 1) == (i >> 5)))
    lora = mm(back, recv_ref[...])
    combined = base_ref[...] + ADAPTER_SCALE * lora
    key = combined[:n]
    half = HD // 2
    turned = jnp.concatenate([key[:, half:], key[:, :half]], 1)
    key = key * cos_ref[...] + turned * sin_ref[...]
    new = jnp.concatenate([key, combined[n:]], 0).astype(BF)
    i, j = iota((2 * n, 2 * n), 0), iota((2 * n, 2 * n), 1)
    new_ref[...] = mm(onehot((i & 1) * n + (i >> 1) == j), new).astype(BF)
    key = new[:n].astype(F32)
    value = new[n:].astype(F32)
    for h in range(heads):
        rows = slice(h * n, (h + 1) * n)
        q = q_ref[:, h * HD : (h + 1) * HD].astype(F32)
        own = jnp.sum(q * key, 1, keepdims=True) * (1.0 / math.sqrt(HD))
        top = cache_ref[1, rows, :]
        high = jnp.maximum(top, own)
        old = jnp.exp(top - high)
        mine = jnp.exp(own - high)
        mixed = cache_ref[0, rows, :] * old + mine * value
        att_ref[:, h * HD : (h + 1) * HD] = (mixed / (cache_ref[2, rows, :] * old + mine)).astype(BF)


def shape(dims, dtype):
    return jax.ShapeDtypeStruct(dims, dtype)


def per_device(
    hidden, queries, w_kv, adapters_down, adapters_up, kv_pages, tenant_ids, owner_table, page_tables, lengths
):
    n = hidden.shape[0]
    width = hidden.shape[1]

    def swap_core(a):
        return lax.ppermute(a, "tp", [(i, i ^ 1) for i in range(8)])

    def along_y(a):
        return [
            lax.ppermute(a, "tp", [(i, ((i // 2 + d) % 4) * 2 + i % 2) for i in range(8)])
            for d in (1, 2, 3)
        ]

    entries = owner_table.shape[0]
    send, dest, own = call(
        route_body,
        (shape((n * CHUNK, HD), BF), shape((n, HD), F32), shape((n, width), BF)),
        3,
        2 * 576 * 256 * 128,
        300000,
        scratch=(
            pltpu.VMEM((n, width), BF),
            pltpu.VMEM((1, n), I32),
            pltpu.VMEM((1, entries), I32),
            pltpu.SemaphoreType.DMA((3,)),
        ),
        limit=ALL,
        far=(0, 1, 2),
    )(hidden, tenant_ids.reshape(1, -1), owner_table.reshape(1, -1))
    send = send.reshape(n, CHUNK // 2, 2, HD)
    recv = lax.all_to_all(send, "pool", 0, 0, tiled=True).reshape(n * CHUNK, HD)

    other = swap_core(own)
    pair = jnp.stack([own, other])
    far = along_y(pair)
    half = HD // 2
    frequency = 10000.0 ** (-jnp.arange(half, dtype=F32) * 2.0 / HD)
    angles = lengths.astype(F32)[:, None] * frequency
    cosine, sine = jnp.cos(angles), jnp.sin(angles)
    cosine = jnp.concatenate([cosine, cosine], 1)
    sine = jnp.concatenate([-sine, sine], 1)
    pages = kv_pages.reshape(-1, HD)
    tables = page_tables.T
    cache = call(
        cached_body,
        shape((3, 8 * n, HD), F32),
        4,
        4 * 256 * 1024 * 128,
        10000000,
        scratch=(
            pltpu.VMEM((n, width), BF),
            pltpu.VMEM(pages.shape, BF),
            pltpu.VMEM(tables.shape, I32),
            pltpu.VMEM((1, n), I32),
            pltpu.SemaphoreType.DMA((4,)),
        ),
        limit=ALL,
        far=(0, 1, 2, 3),
    )(queries, pages, tables, lengths.reshape(1, -1))
    recv, cache, *far = lax.optimization_barrier((recv, cache, *far))
    part, slot = call(
        down_body,
        (shape((2 * n, HD), F32), shape((2 * n, HD), F32)),
        2,
        2 * 64 * 16 * 1024 * 128,
        4500000,
        scratch=(pltpu.VMEM(adapters_down.shape, BF), pltpu.SemaphoreType.DMA((4,))),
        limit=MOST,
        far=(1,),
    )(recv, adapters_down)
    part = part + swap_core(part)
    sums = along_y(part)
    back = call(up_body, shape((4 * n, HD), BF), 6, 2 * 128 * 2048 * 128, 600000)(
        part, *sums, slot, adapters_up.reshape(-1, HD)
    )
    back = back.reshape(n, 2, 2, HD)
    back = lax.all_to_all(back, "pool", 0, 0, tiled=True).reshape(4 * n, HD)

    me = lax.axis_index("tp").astype(I32).reshape(1)
    base = call(
        base_body,
        shape((2 * n, HD), F32),
        7,
        4 * 64 * 8192 * 128,
        8000000,
        scratch=(pltpu.VMEM((8, 2 * width, HD), BF), pltpu.SemaphoreType.DMA((8,))),
        limit=MOST,
        smem=(0,),
        far=(6,),
    )(me, own, other, *far, w_kv.reshape(-1, HD))

    attention, new_kv = call(
        finish_body, (shape((n, width), BF), shape((2 * n, HD), BF)), 7, 1000000, 1000000
    )(back, dest, base, cosine, sine, queries, cache)
    return attention, new_kv.reshape(n, 2, HD)


def solution(mesh):
    in_specs = (
        P("pool", "tp"),
        P("pool", "tp"),
        P(None, None, "tp"),
        P("pool", "tp", None),
        P("pool", None, None, "tp"),
        P("pool", None, None, "tp"),
        P("pool"),
        P(),
        P("pool", None),
        P("pool"),
    )
    out_specs = (P("pool", "tp"), P("pool", None, "tp"))
    return jax.shard_map(
        per_device, mesh=mesh, in_specs=in_specs, out_specs=out_specs, check_vma=False
    )
```

```python
import math

import jax
import jax.numpy as jnp
from jax import lax
from jax.experimental import pallas as pl
from jax.experimental.pallas import tpu as pltpu
from jax.sharding import PartitionSpec as P

HD = 128
ADAPTER_SCALE = 0.5
BF = jnp.bfloat16
F32 = jnp.float32
I32 = jnp.int32
VMEM = pl.BlockSpec(memory_space=pltpu.VMEM)
SMEM = pl.BlockSpec(memory_space=pltpu.SMEM)
HBM = pl.BlockSpec(memory_space=pl.ANY)
ALL = 58
MOST = 52
CHUNK = 18


def iota(shape, dim):
    return lax.broadcasted_iota(I32, shape, dim)


def mm(a, b):
    return jnp.dot(a, b, preferred_element_type=F32)


def mm_t(a, b):
    return lax.dot_general(a, b, (((1,), (1,)), ((), ())), preferred_element_type=F32)


def onehot(mask):
    return jnp.where(mask, 1.0, 0.0).astype(BF)


def column(row, n):
    return jnp.sum(jnp.where(iota((n, n), 0) == iota((n, n), 1), row, 0.0), 1, keepdims=True)


def chunked(x):
    return jnp.concatenate([x[:, i * HD : (i + 1) * HD] for i in range(x.shape[1] // HD)], 0)


def call(body, outs, n_in, flops=0, read=0, scratch=(), limit=16, smem=(), far=()):
    return pl.pallas_call(
        body,
        out_shape=outs,
        in_specs=[SMEM if i in smem else HBM if i in far else VMEM for i in range(n_in)],
        out_specs=jax.tree.map(lambda _: VMEM, outs),
        scratch_shapes=scratch,
        compiler_params=pltpu.CompilerParams(vmem_limit_bytes=limit << 20),
        cost_estimate=pl.CostEstimate(flops=flops, bytes_accessed=read, transcendentals=0),
    )


def fetch(sources, targets, sems):
    copies = [
        pltpu.make_async_copy(source, target, sems.at[i])
        for i, (source, target) in enumerate(zip(sources, targets))
    ]
    for copy in copies:
        copy.start()
    return copies


def route_body(
    hidden_at, tenants_at, table_at, send_ref, dest_ref, hidden_ref, tenants_ref, table_ref, sems
):
    copies = fetch(
        (tenants_at, table_at, hidden_at), (tenants_ref, table_ref, hidden_ref), sems
    )
    copies[0].wait()
    copies[1].wait()
    n = tenants_ref.shape[1]
    tenant = column(tenants_ref[...].astype(F32), n)
    entries = table_ref.shape[1]
    table = table_ref[...].astype(F32)
    lanes = iota((n, entries), 1).astype(F32)
    storage = jnp.sum(jnp.where(tenant == lanes, table, 0.0), 1, keepdims=True).astype(I32)
    owner = (storage >> 4).astype(F32)
    slot = (storage & 15).astype(F32)
    eye = iota((n, n), 0) == iota((n, n), 1)
    owner_row = jnp.sum(jnp.where(eye, owner, 0.0), 0, keepdims=True)
    same = (owner == owner_row) & (iota((n, n), 1) < iota((n, n), 0))
    rank = jnp.sum(jnp.where(same, 1.0, 0.0), 1, keepdims=True)
    dest = owner * 2.0 + rank
    dest_ref[...] = jnp.broadcast_to(dest, dest_ref.shape)
    wide = (iota((n, 8 * n), 1) & (n - 1)) == iota((n, 8 * n), 0)
    dest_wide = jnp.sum(jnp.where(wide, dest, 0.0), 0, keepdims=True).astype(I32)
    dest_row = dest_wide[:, :n]
    i = iota((CHUNK * n, 1), 0)
    chunk = (i * 3641) >> 16
    rest = i - CHUNK * chunk
    place, part = chunk * 2 + (rest & 1), rest >> 1
    where_from = iota((1, 8 * n), 1)
    pick = onehot((place == dest_wide) & (part == (where_from >> 5)))
    pick_slot = onehot((place == dest_row) & (part == 8))
    slots = jnp.broadcast_to(slot, (n, HD)).astype(BF)
    sent = mm(pick_slot, slots)
    copies[2].wait()
    send_ref[...] = (sent + mm(pick, chunked(hidden_ref[...]))).astype(BF)


def down_body(*refs):
    recv_ref, down_at = refs[:2]
    part_ref, slot_ref, down_ref, sems = refs[-4:]
    count = down_ref.shape[0]
    parts = sems.shape[0]
    each = count // parts
    pieces = [slice(k * each, (k + 1) * each) for k in range(parts)]
    copies = fetch([down_at.at[p] for p in pieces], [down_ref.at[p] for p in pieces], sems)
    n = recv_ref.shape[0] // CHUNK
    m = 2 * n
    rows = recv_ref[...]
    i, j = iota((8 * m, 1), 0), iota((1, CHUNK * n), 1)
    order = onehot(((i & (m - 1)) >> 1) * CHUNK + (i >> 6) * 2 + (i & 1) == j)
    x = mm(order, rows).astype(BF)
    x = jnp.concatenate([x[c * m : (c + 1) * m] for c in range(8)], 1)
    i = iota((m, 1), 0)
    slot = mm(onehot((i >> 1) * CHUNK + 16 + (i & 1) == j), rows)
    slot_ref[...] = slot
    total = jnp.zeros((m, HD), F32)
    for a in range(0, count, 2):
        if a % each == 0:
            copies[a // each].wait()
        y = mm(x, jnp.concatenate([down_ref[a], down_ref[a + 1]], 1))
        total = total + jnp.where(slot == a, y[:, :HD], 0.0)
        total = total + jnp.where(slot == a + 1, y[:, HD:], 0.0)
    part_ref[...] = total


def up_body(p0_ref, p1_ref, p2_ref, p3_ref, slot_ref, up_ref, send_ref):
    m = slot_ref.shape[0]
    down = (p0_ref[...] + p1_ref[...]) + (p2_ref[...] + p3_ref[...])
    first = iota((m, HD), 1) < HD // 2
    both = jnp.concatenate([jnp.where(first, down, 0.0), jnp.where(first, 0.0, down)], 0)
    slot = jnp.concatenate([slot_ref[...]] * 2, 0)
    count = up_ref.shape[0] // HD
    picked = jnp.concatenate(
        [jnp.where(slot == a, both, 0.0).astype(BF) for a in range(count)], 1
    )
    lora = mm(picked, up_ref[...])
    i, j = iota((2 * m, 1), 0), iota((1, 2 * m), 1)
    order = onehot((i & 1) * m + (i >> 1) == j)
    send_ref[...] = mm(order, lora.astype(BF)).astype(BF)


def attend_cached(q_ref, pages_ref, tables_ref, lengths_ref, cache_ref, score_ref, weight_ref):
    n = q_ref.shape[0]
    heads = q_ref.shape[1] // HD
    page = HD
    count = pages_ref.shape[0] // (2 * page)
    tokens = count * page
    i, j = iota((2 * page, 2 * page), 0), iota((2 * page, 2 * page), 1)
    part = onehot((i & (page - 1)) * 2 + (i >> 7) == j)
    q = chunked(q_ref[...])
    values = []
    for p in range(count):
        both = mm(part, pages_ref[p * 2 * page : (p + 1) * 2 * page, :]).astype(BF)
        score_ref[:, p * page : (p + 1) * page] = mm_t(q, both[:page])
        values.append(both[page:])
    values = jnp.concatenate(values, 0)
    eye = onehot(iota((n, n), 0) == iota((n, n), 1))
    tables = mm_t(eye, tables_ref[...].astype(F32).astype(BF)).astype(I32)
    length = column(lengths_ref[...].astype(F32), n).astype(I32)
    at = iota((n, tokens), 1)
    page_id, place = at >> 7, at & (page - 1)
    counts = jnp.zeros((n, tokens), F32)
    for j in range(tables_ref.shape[0]):
        hit = (tables[:, j : j + 1] == page_id) & (place < length - j * page)
        counts = counts + jnp.where(hit, 1.0, 0.0)
    for h in range(heads):
        rows = slice(h * n, (h + 1) * n)
        scores = score_ref[rows, :] * (1.0 / math.sqrt(HD))
        scores = jnp.where(counts > 0.0, scores, -jnp.inf)
        top = jnp.max(scores, 1, keepdims=True)
        weights = jnp.exp(scores - top) * counts
        weight_ref[rows, :] = weights.astype(BF)
        cache_ref[1, rows, :] = jnp.broadcast_to(top, (n, HD))
        cache_ref[2, rows, :] = jnp.broadcast_to(jnp.sum(weights, 1, keepdims=True), (n, HD))
    cache_ref[0] = mm(weight_ref[...], values)


def wait_body(
    index_ref,
    x0_ref,
    x1_ref,
    y1_ref,
    y2_ref,
    y3_ref,
    q_ref,
    pages_ref,
    tables_ref,
    lengths_ref,
    w_at,
    base_ref,
    cache_ref,
    w_ref,
    score_ref,
    weight_ref,
    sems,
):
    me = index_ref[0]
    n = x0_ref.shape[0]
    width = x0_ref.shape[1]
    away = [(dy, dc) for dy in range(4) for dc in range(2)]
    spots = []
    for dy, dc in away:
        peer = (((me >> 1) + 4 - dy) & 3) * 2 + ((me & 1) ^ dc)
        spots.append(pl.ds(pl.multiple_of(peer * (2 * width), 2 * width), 2 * width))
    copies = fetch([w_at.at[p] for p in spots], [w_ref.at[k] for k in range(8)], sems)
    attend_cached(q_ref, pages_ref, tables_ref, lengths_ref, cache_ref, score_ref, weight_ref)
    chunks = width // HD
    i, j = iota((HD, 4 * HD), 0), iota((HD, 4 * HD), 1)
    spread = onehot((j & 255) == 2 * i + (j >> 8))
    total = jnp.zeros((2 * n, HD), F32)
    for k, (dy, dc) in enumerate(away):
        if dy == 0:
            x = (x0_ref, x1_ref)[dc][...]
        else:
            x = (y1_ref, y2_ref, y3_ref)[dy - 1][dc]
        e = mm(chunked(x), spread).astype(BF)
        both = jnp.concatenate(
            [
                jnp.concatenate(
                    [e[g * n : (g + 1) * n, c * 256 : (c + 1) * 256] for g in range(chunks)], 1
                )
                for c in range(2)
            ],
            0,
        )
        copies[k].wait()
        total = total + mm(both, w_ref[k])
    base_ref[...] = total


def finish_body(
    recv_ref, dest_ref, base_ref, cos_ref, sin_ref, q_ref, cache_ref, att_ref, new_ref
):
    n = q_ref.shape[0]
    heads = q_ref.shape[1] // HD
    dest = dest_ref[...].astype(I32)
    dest = jnp.concatenate([dest, dest], 0)
    i, j = iota((2 * n, 1), 0), iota((1, 4 * n), 1)
    back = onehot((dest == (j >> 1)) & ((j & 1) == (i >> 5)))
    lora = mm(back, recv_ref[...])
    combined = base_ref[...] + ADAPTER_SCALE * lora
    key = combined[:n]
    half = HD // 2
    turned = jnp.concatenate([key[:, half:], key[:, :half]], 1)
    key = key * cos_ref[...] + turned * sin_ref[...]
    new = jnp.concatenate([key, combined[n:]], 0).astype(BF)
    i, j = iota((2 * n, 2 * n), 0), iota((2 * n, 2 * n), 1)
    new_ref[...] = mm(onehot((i & 1) * n + (i >> 1) == j), new).astype(BF)
    key = new[:n].astype(F32)
    value = new[n:].astype(F32)
    for h in range(heads):
        rows = slice(h * n, (h + 1) * n)
        q = q_ref[:, h * HD : (h + 1) * HD].astype(F32)
        own = jnp.sum(q * key, 1, keepdims=True) * (1.0 / math.sqrt(HD))
        top = cache_ref[1, rows, :]
        high = jnp.maximum(top, own)
        old = jnp.exp(top - high)
        mine = jnp.exp(own - high)
        mixed = cache_ref[0, rows, :] * old + mine * value
        att_ref[:, h * HD : (h + 1) * HD] = (mixed / (cache_ref[2, rows, :] * old + mine)).astype(BF)


def shape(dims, dtype):
    return jax.ShapeDtypeStruct(dims, dtype)


def per_device(
    hidden, queries, w_kv, adapters_down, adapters_up, kv_pages, tenant_ids, owner_table, page_tables, lengths
):
    n = hidden.shape[0]
    width = hidden.shape[1]

    def swap_core(a):
        return lax.ppermute(a, "tp", [(i, i ^ 1) for i in range(8)])

    def along_y(a):
        return [
            lax.ppermute(a, "tp", [(i, ((i // 2 + d) % 4) * 2 + i % 2) for i in range(8)])
            for d in (1, 2, 3)
        ]

    entries = owner_table.shape[0]
    send, dest = call(
        route_body,
        (shape((n * CHUNK, HD), BF), shape((n, HD), F32)),
        3,
        2 * 576 * 256 * 128,
        300000,
        scratch=(
            pltpu.VMEM((n, width), BF),
            pltpu.VMEM((1, n), I32),
            pltpu.VMEM((1, entries), I32),
            pltpu.SemaphoreType.DMA((3,)),
        ),
        limit=ALL,
        far=(0, 1, 2),
    )(hidden, tenant_ids.reshape(1, -1), owner_table.reshape(1, -1))
    send, hidden = lax.optimization_barrier((send, hidden))
    send = send.reshape(n, CHUNK // 2, 2, HD)
    recv = lax.all_to_all(send, "pool", 0, 0, tiled=True).reshape(n * CHUNK, HD)

    other = swap_core(hidden)
    far = along_y(jnp.stack([hidden, other]))
    recv, *far = lax.optimization_barrier((recv, *far))

    part, slot = call(
        down_body,
        (shape((2 * n, HD), F32), shape((2 * n, HD), F32)),
        2,
        2 * 64 * 16 * 1024 * 128,
        4500000,
        scratch=(pltpu.VMEM(adapters_down.shape, BF), pltpu.SemaphoreType.DMA((4,))),
        limit=MOST,
        far=(1,),
    )(recv, adapters_down)
    part = part + swap_core(part)
    sums = along_y(part)
    back = call(up_body, shape((4 * n, HD), BF), 6, 2 * 128 * 2048 * 128, 600000)(
        part, *sums, slot, adapters_up.reshape(-1, HD)
    )
    back, *far = lax.optimization_barrier((back, *far))
    back = back.reshape(n, 2, 2, HD)
    back = lax.all_to_all(back, "pool", 0, 0, tiled=True).reshape(4 * n, HD)

    half = HD // 2
    frequency = 10000.0 ** (-jnp.arange(half, dtype=F32) * 2.0 / HD)
    angles = lengths.astype(F32)[:, None] * frequency
    cosine, sine = jnp.cos(angles), jnp.sin(angles)
    cosine = jnp.concatenate([cosine, cosine], 1)
    sine = jnp.concatenate([-sine, sine], 1)
    pages = kv_pages.reshape(-1, HD)
    tokens = pages.shape[0] // 2
    me = lax.axis_index("tp").astype(I32).reshape(1)
    base, cache = call(
        wait_body,
        (shape((2 * n, HD), F32), shape((3, 8 * n, HD), F32)),
        11,
        4 * 64 * 8192 * 128 + 4 * 256 * 1024 * 128,
        16000000,
        scratch=(
            pltpu.VMEM((8, 2 * width, HD), BF),
            pltpu.VMEM((8 * n, tokens), F32),
            pltpu.VMEM((8 * n, tokens), BF),
            pltpu.SemaphoreType.DMA((8,)),
        ),
        limit=MOST,
        smem=(0,),
        far=(10,),
    )(
        me,
        hidden,
        other,
        *far,
        queries,
        pages,
        page_tables.T,
        lengths.reshape(1, -1),
        w_kv.reshape(-1, HD),
    )

    attention, new_kv = call(
        finish_body, (shape((n, width), BF), shape((2 * n, HD), BF)), 7, 1000000, 1000000
    )(back, dest, base, cosine, sine, queries, cache)
    return attention, new_kv.reshape(n, 2, HD)


def solution(mesh):
    in_specs = (
        P("pool", "tp"),
        P("pool", "tp"),
        P(None, None, "tp"),
        P("pool", "tp", None),
        P("pool", None, None, "tp"),
        P("pool", None, None, "tp"),
        P("pool"),
        P(),
        P("pool", None),
        P("pool"),
    )
    out_specs = (P("pool", "tp"), P("pool", None, "tp"))
    return jax.shard_map(
        per_device, mesh=mesh, in_specs=in_specs, out_specs=out_specs, check_vma=False
    )
```

```python
import math

import jax
import jax.numpy as jnp
from jax import lax
from jax.experimental import pallas as pl
from jax.experimental.pallas import tpu as pltpu
from jax.sharding import PartitionSpec as P

HD = 128
ADAPTER_SCALE = 0.5
BF = jnp.bfloat16
F32 = jnp.float32
I32 = jnp.int32
VMEM = pl.BlockSpec(memory_space=pltpu.VMEM)
SMEM = pl.BlockSpec(memory_space=pltpu.SMEM)
HBM = pl.BlockSpec(memory_space=pl.ANY)
ALL = 58
MOST = 52
EARLY = 6
CHUNK = 18


def iota(shape, dim):
    return lax.broadcasted_iota(I32, shape, dim)


def mm(a, b):
    return jnp.dot(a, b, preferred_element_type=F32)


def mm_t(a, b):
    return lax.dot_general(a, b, (((1,), (1,)), ((), ())), preferred_element_type=F32)


def onehot(mask):
    return jnp.where(mask, 1.0, 0.0).astype(BF)


def column(row, n):
    return jnp.sum(jnp.where(iota((n, n), 0) == iota((n, n), 1), row, 0.0), 1, keepdims=True)


def chunked(x):
    return jnp.concatenate([x[:, i * HD : (i + 1) * HD] for i in range(x.shape[1] // HD)], 0)


def call(body, outs, n_in, flops=0, read=0, scratch=(), limit=16, smem=(), far=()):
    return pl.pallas_call(
        body,
        out_shape=outs,
        in_specs=[SMEM if i in smem else HBM if i in far else VMEM for i in range(n_in)],
        out_specs=jax.tree.map(lambda _: VMEM, outs),
        scratch_shapes=scratch,
        compiler_params=pltpu.CompilerParams(vmem_limit_bytes=limit << 20),
        cost_estimate=pl.CostEstimate(flops=flops, bytes_accessed=read, transcendentals=0),
    )


def fetch(sources, targets, sems):
    copies = [
        pltpu.make_async_copy(source, target, sems.at[i])
        for i, (source, target) in enumerate(zip(sources, targets))
    ]
    for copy in copies:
        copy.start()
    return copies


def route_body(
    hidden_at, tenants_at, table_at, send_ref, dest_ref, hidden_ref, tenants_ref, table_ref, sems
):
    copies = fetch(
        (tenants_at, table_at, hidden_at), (tenants_ref, table_ref, hidden_ref), sems
    )
    copies[0].wait()
    copies[1].wait()
    n = tenants_ref.shape[1]
    tenant = column(tenants_ref[...].astype(F32), n)
    entries = table_ref.shape[1]
    table = table_ref[...].astype(F32)
    lanes = iota((n, entries), 1).astype(F32)
    storage = jnp.sum(jnp.where(tenant == lanes, table, 0.0), 1, keepdims=True).astype(I32)
    owner = (storage >> 4).astype(F32)
    slot = (storage & 15).astype(F32)
    eye = iota((n, n), 0) == iota((n, n), 1)
    owner_row = jnp.sum(jnp.where(eye, owner, 0.0), 0, keepdims=True)
    same = (owner == owner_row) & (iota((n, n), 1) < iota((n, n), 0))
    rank = jnp.sum(jnp.where(same, 1.0, 0.0), 1, keepdims=True)
    dest = owner * 2.0 + rank
    dest_ref[...] = jnp.broadcast_to(dest, dest_ref.shape)
    wide = (iota((n, 8 * n), 1) & (n - 1)) == iota((n, 8 * n), 0)
    dest_wide = jnp.sum(jnp.where(wide, dest, 0.0), 0, keepdims=True).astype(I32)
    dest_row = dest_wide[:, :n]
    i = iota((CHUNK * n, 1), 0)
    chunk = (i * 3641) >> 16
    rest = i - CHUNK * chunk
    place, part = chunk * 2 + (rest & 1), rest >> 1
    where_from = iota((1, 8 * n), 1)
    pick = onehot((place == dest_wide) & (part == (where_from >> 5)))
    pick_slot = onehot((place == dest_row) & (part == 8))
    slots = jnp.broadcast_to(slot, (n, HD)).astype(BF)
    sent = mm(pick_slot, slots)
    copies[2].wait()
    send_ref[...] = (sent + mm(pick, chunked(hidden_ref[...]))).astype(BF)


def early_body(down_at, first_ref, sem):
    copy = pltpu.make_async_copy(down_at.at[: first_ref.shape[0]], first_ref, sem)
    copy.start()
    copy.wait()


def down_body(*refs):
    recv_ref, first_ref, down_at, part_ref, slot_ref, down_ref, sems = refs
    early = first_ref.shape[0]
    each = 2
    pieces = [slice(k, k + each) for k in range(0, down_ref.shape[0], each)]
    copies = fetch(
        [down_at.at[early + p.start : early + p.stop] for p in pieces],
        [down_ref.at[p] for p in pieces],
        sems,
    )
    n = recv_ref.shape[0] // CHUNK
    m = 2 * n
    rows = recv_ref[...]
    i, j = iota((8 * m, 1), 0), iota((1, CHUNK * n), 1)
    order = onehot(((i & (m - 1)) >> 1) * CHUNK + (i >> 6) * 2 + (i & 1) == j)
    x = mm(order, rows).astype(BF)
    x = jnp.concatenate([x[c * m : (c + 1) * m] for c in range(8)], 1)
    i = iota((m, 1), 0)
    slot = mm(onehot((i >> 1) * CHUNK + 16 + (i & 1) == j), rows)
    slot_ref[...] = slot
    total = jnp.zeros((m, HD), F32)
    for a in range(0, down_at.shape[0], each):
        if a < early:
            pair = first_ref[a], first_ref[a + 1]
        else:
            copies[(a - early) // each].wait()
            pair = down_ref[a - early], down_ref[a - early + 1]
        y = mm(x, jnp.concatenate(pair, 1))
        total = total + jnp.where(slot == a, y[:, :HD], 0.0)
        total = total + jnp.where(slot == a + 1, y[:, HD:], 0.0)
    part_ref[...] = total


def up_body(p0_ref, p1_ref, p2_ref, p3_ref, slot_ref, up_ref, send_ref):
    m = slot_ref.shape[0]
    down = (p0_ref[...] + p1_ref[...]) + (p2_ref[...] + p3_ref[...])
    first = iota((m, HD), 1) < HD // 2
    both = jnp.concatenate([jnp.where(first, down, 0.0), jnp.where(first, 0.0, down)], 0)
    slot = jnp.concatenate([slot_ref[...]] * 2, 0)
    count = up_ref.shape[0] // HD
    picked = jnp.concatenate(
        [jnp.where(slot == a, both, 0.0).astype(BF) for a in range(count)], 1
    )
    lora = mm(picked, up_ref[...])
    i, j = iota((2 * m, 1), 0), iota((1, 2 * m), 1)
    order = onehot((i & 1) * m + (i >> 1) == j)
    send_ref[...] = mm(order, lora.astype(BF)).astype(BF)


def attend_cached(q_ref, pages_ref, tables_ref, lengths_ref, cache_ref):
    n = q_ref.shape[0]
    heads = q_ref.shape[1] // HD
    page = HD
    count = pages_ref.shape[0] // (2 * page)
    tokens = count * page
    eye = onehot(iota((n, n), 0) == iota((n, n), 1))
    tables = mm_t(eye, tables_ref[...].astype(F32).astype(BF)).astype(I32)
    length = column(lengths_ref[...].astype(F32), n).astype(I32)
    at = iota((n, tokens), 1)
    page_id, place = at >> 7, at & (page - 1)
    counts = jnp.zeros((n, tokens), F32)
    for j in range(tables_ref.shape[0]):
        hit = (tables[:, j : j + 1] == page_id) & (place < length - j * page)
        counts = counts + jnp.where(hit, 1.0, 0.0)
    i, j = iota((2 * page, 2 * page), 0), iota((2 * page, 2 * page), 1)
    part = onehot((i & (page - 1)) * 2 + (i >> 7) == j)
    keys, values = [], []
    for p in range(count):
        both = mm(part, pages_ref[p * 2 * page : (p + 1) * 2 * page, :]).astype(BF)
        keys.append(both[:page])
        values.append(both[page:])
    keys = jnp.concatenate(keys, 0)
    values = jnp.concatenate(values, 0)
    for h in range(heads):
        scores = mm_t(q_ref[:, h * HD : (h + 1) * HD], keys) * (1.0 / math.sqrt(HD))
        scores = jnp.where(counts > 0.0, scores, -jnp.inf)
        top = jnp.max(scores, 1, keepdims=True)
        weights = jnp.exp(scores - top) * counts
        rows = slice(h * n, (h + 1) * n)
        cache_ref[0, rows, :] = mm(weights.astype(BF), values)
        cache_ref[1, rows, :] = jnp.broadcast_to(top, (n, HD))
        cache_ref[2, rows, :] = jnp.broadcast_to(jnp.sum(weights, 1, keepdims=True), (n, HD))


def wait_body(
    index_ref,
    mine_ref,
    other_ref,
    q_ref,
    pages_ref,
    tables_ref,
    lengths_ref,
    w_at,
    base_ref,
    cache_ref,
    w_ref,
    sems,
):
    me = index_ref[0]
    _, n, width = mine_ref.shape
    away = [(dy, dc) for dy in range(4) for dc in range(2)]
    spots = []
    for dy, dc in away:
        peer = (((me >> 1) + 4 - dy) & 3) * 2 + ((me & 1) ^ dc)
        spots.append(pl.ds(pl.multiple_of(peer * (2 * width), 2 * width), 2 * width))
    copies = fetch([w_at.at[p] for p in spots], [w_ref.at[k] for k in range(8)], sems)
    attend_cached(q_ref, pages_ref, tables_ref, lengths_ref, cache_ref)
    chunks = width // HD
    i, j = iota((HD, 4 * HD), 0), iota((HD, 4 * HD), 1)
    spread = onehot((j & 255) == 2 * i + (j >> 8))
    total = jnp.zeros((2 * n, HD), F32)
    for k, (dy, dc) in enumerate(away):
        x = (mine_ref, other_ref)[dc][dy]
        e = mm(chunked(x), spread).astype(BF)
        both = jnp.concatenate(
            [
                jnp.concatenate(
                    [e[g * n : (g + 1) * n, c * 256 : (c + 1) * 256] for g in range(chunks)], 1
                )
                for c in range(2)
            ],
            0,
        )
        copies[k].wait()
        total = total + mm(both, w_ref[k])
    base_ref[...] = total


def finish_body(
    recv_ref, dest_ref, base_ref, cos_ref, sin_ref, q_ref, cache_ref, att_ref, new_ref
):
    n = q_ref.shape[0]
    heads = q_ref.shape[1] // HD
    dest = dest_ref[...].astype(I32)
    dest = jnp.concatenate([dest, dest], 0)
    i, j = iota((2 * n, 1), 0), iota((1, 4 * n), 1)
    back = onehot((dest == (j >> 1)) & ((j & 1) == (i >> 5)))
    lora = mm(back, recv_ref[...])
    combined = base_ref[...] + ADAPTER_SCALE * lora
    key = combined[:n]
    half = HD // 2
    turned = jnp.concatenate([key[:, half:], key[:, :half]], 1)
    key = key * cos_ref[...] + turned * sin_ref[...]
    new = jnp.concatenate([key, combined[n:]], 0).astype(BF)
    i, j = iota((2 * n, 2 * n), 0), iota((2 * n, 2 * n), 1)
    new_ref[...] = mm(onehot((i & 1) * n + (i >> 1) == j), new).astype(BF)
    key = new[:n].astype(F32)
    value = new[n:].astype(F32)
    for h in range(heads):
        rows = slice(h * n, (h + 1) * n)
        q = q_ref[:, h * HD : (h + 1) * HD].astype(F32)
        own = jnp.sum(q * key, 1, keepdims=True) * (1.0 / math.sqrt(HD))
        top = cache_ref[1, rows, :]
        high = jnp.maximum(top, own)
        old = jnp.exp(top - high)
        mine = jnp.exp(own - high)
        mixed = cache_ref[0, rows, :] * old + mine * value
        att_ref[:, h * HD : (h + 1) * HD] = (mixed / (cache_ref[2, rows, :] * old + mine)).astype(BF)


def shape(dims, dtype):
    return jax.ShapeDtypeStruct(dims, dtype)


def per_device(
    hidden, queries, w_kv, adapters_down, adapters_up, kv_pages, tenant_ids, owner_table, page_tables, lengths
):
    n = hidden.shape[0]
    width = hidden.shape[1]

    def swap_core(a):
        return lax.ppermute(a, "tp", [(i, i ^ 1) for i in range(8)])

    def along_y(a):
        return [
            lax.ppermute(a, "tp", [(i, ((i // 2 + d) % 4) * 2 + i % 2) for i in range(8)])
            for d in (1, 2, 3)
        ]

    entries = owner_table.shape[0]
    send, dest = call(
        route_body,
        (shape((n * CHUNK, HD), BF), shape((n, HD), F32)),
        3,
        2 * 576 * 256 * 128,
        300000,
        scratch=(
            pltpu.VMEM((n, width), BF),
            pltpu.VMEM((1, n), I32),
            pltpu.VMEM((1, entries), I32),
            pltpu.SemaphoreType.DMA((3,)),
        ),
        limit=ALL,
        far=(0, 1, 2),
    )(hidden, tenant_ids.reshape(1, -1), owner_table.reshape(1, -1))
    send, lengths = lax.optimization_barrier((send, lengths))
    send = send.reshape(n, CHUNK // 2, 2, HD)
    recv = lax.all_to_all(send, "pool", 0, 0, tiled=True).reshape(n * CHUNK, HD)

    half = HD // 2
    frequency = 10000.0 ** (-jnp.arange(half, dtype=F32) * 2.0 / HD)
    angles = lengths.astype(F32)[:, None] * frequency
    cosine, sine = jnp.cos(angles), jnp.sin(angles)
    cosine = jnp.concatenate([cosine, cosine], 1)
    sine = jnp.concatenate([-sine, sine], 1)
    cosine, sine, hidden = lax.optimization_barrier((cosine, sine, hidden))

    far = along_y(hidden)
    count = adapters_down.shape[0]
    early = EARLY
    first = call(
        early_body,
        shape((early, *adapters_down.shape[1:]), BF),
        1,
        0,
        8000000,
        scratch=(pltpu.SemaphoreType.DMA,),
        limit=MOST,
        far=(0,),
    )(adapters_down)
    recv, first, *far = lax.optimization_barrier((recv, first, *far))

    part, slot = call(
        down_body,
        (shape((2 * n, HD), F32), shape((2 * n, HD), F32)),
        3,
        2 * 64 * 16 * 1024 * 128,
        4500000,
        scratch=(
            pltpu.VMEM((count - early, *adapters_down.shape[1:]), BF),
            pltpu.SemaphoreType.DMA(((count - early) // 2,)),
        ),
        limit=MOST,
        far=(2,),
    )(recv, first, adapters_down)
    part = part + swap_core(part)
    part, *far = lax.optimization_barrier((part, *far))
    sums = along_y(part)
    mine = jnp.stack([hidden, *far])
    mine, *sums = lax.optimization_barrier((mine, *sums))
    back = call(up_body, shape((4 * n, HD), BF), 6, 2 * 128 * 2048 * 128, 600000)(
        part, *sums, slot, adapters_up.reshape(-1, HD)
    )
    back, mine = lax.optimization_barrier((back, mine))
    other = swap_core(mine)
    back = back.reshape(n, 2, 2, HD)
    back = lax.all_to_all(back, "pool", 0, 0, tiled=True).reshape(4 * n, HD)

    pages = kv_pages.reshape(-1, HD)
    me = lax.axis_index("tp").astype(I32).reshape(1)
    base, cache = call(
        wait_body,
        (shape((2 * n, HD), F32), shape((3, 8 * n, HD), F32)),
        8,
        4 * 64 * 8192 * 128 + 4 * 256 * 1024 * 128,
        16000000,
        scratch=(
            pltpu.VMEM((8, 2 * width, HD), BF),
            pltpu.SemaphoreType.DMA((8,)),
        ),
        limit=MOST,
        smem=(0,),
        far=(7,),
    )(
        me,
        mine,
        other,
        queries,
        pages,
        page_tables.T,
        lengths.reshape(1, -1),
        w_kv.reshape(-1, HD),
    )

    attention, new_kv = call(
        finish_body, (shape((n, width), BF), shape((2 * n, HD), BF)), 7, 1000000, 1000000
    )(back, dest, base, cosine, sine, queries, cache)
    return attention, new_kv.reshape(n, 2, HD)


def solution(mesh):
    in_specs = (
        P("pool", "tp"),
        P("pool", "tp"),
        P(None, None, "tp"),
        P("pool", "tp", None),
        P("pool", None, None, "tp"),
        P("pool", None, None, "tp"),
        P("pool"),
        P(),
        P("pool", None),
        P("pool"),
    )
    out_specs = (P("pool", "tp"), P("pool", None, "tp"))
    return jax.shard_map(
        per_device, mesh=mesh, in_specs=in_specs, out_specs=out_specs, check_vma=False
    )
```

```python
import math

import jax
import jax.numpy as jnp
from jax import lax
from jax.experimental import pallas as pl
from jax.experimental.pallas import tpu as pltpu
from jax.sharding import PartitionSpec as P

HD = 128
ADAPTER_SCALE = 0.5
BF = jnp.bfloat16
F32 = jnp.float32
I32 = jnp.int32
VMEM = pl.BlockSpec(memory_space=pltpu.VMEM)
SMEM = pl.BlockSpec(memory_space=pltpu.SMEM)
HBM = pl.BlockSpec(memory_space=pl.ANY)
ALL = 58
MOST = 52
CHUNK = 18


def iota(shape, dim):
    return lax.broadcasted_iota(I32, shape, dim)


def mm(a, b):
    return jnp.dot(a, b, preferred_element_type=F32)


def mm_t(a, b):
    return lax.dot_general(a, b, (((1,), (1,)), ((), ())), preferred_element_type=F32)


def onehot(mask):
    return jnp.where(mask, 1.0, 0.0).astype(BF)


def column(row, n):
    return jnp.sum(jnp.where(iota((n, n), 0) == iota((n, n), 1), row, 0.0), 1, keepdims=True)


def chunked(x):
    return jnp.concatenate([x[:, i * HD : (i + 1) * HD] for i in range(x.shape[1] // HD)], 0)


def call(body, outs, n_in, flops=0, read=0, scratch=(), limit=16, smem=(), far=()):
    return pl.pallas_call(
        body,
        out_shape=outs,
        in_specs=[SMEM if i in smem else HBM if i in far else VMEM for i in range(n_in)],
        out_specs=jax.tree.map(lambda _: VMEM, outs),
        scratch_shapes=scratch,
        compiler_params=pltpu.CompilerParams(vmem_limit_bytes=limit << 20),
        cost_estimate=pl.CostEstimate(flops=flops, bytes_accessed=read, transcendentals=0),
    )


def fetch(sources, targets, sems):
    copies = [
        pltpu.make_async_copy(source, target, sems.at[i])
        for i, (source, target) in enumerate(zip(sources, targets))
    ]
    for copy in copies:
        copy.start()
    return copies


def route_body(
    hidden_at, tenants_at, table_at, send_ref, dest_ref, hidden_ref, tenants_ref, table_ref, sems
):
    copies = fetch(
        (tenants_at, table_at, hidden_at), (tenants_ref, table_ref, hidden_ref), sems
    )
    copies[0].wait()
    copies[1].wait()
    n = tenants_ref.shape[1]
    tenant = column(tenants_ref[...].astype(F32), n)
    entries = table_ref.shape[1]
    table = table_ref[...].astype(F32)
    lanes = iota((n, entries), 1).astype(F32)
    storage = jnp.sum(jnp.where(tenant == lanes, table, 0.0), 1, keepdims=True).astype(I32)
    owner = (storage >> 4).astype(F32)
    slot = (storage & 15).astype(F32)
    eye = iota((n, n), 0) == iota((n, n), 1)
    owner_row = jnp.sum(jnp.where(eye, owner, 0.0), 0, keepdims=True)
    same = (owner == owner_row) & (iota((n, n), 1) < iota((n, n), 0))
    rank = jnp.sum(jnp.where(same, 1.0, 0.0), 1, keepdims=True)
    dest = owner * 2.0 + rank
    dest_ref[...] = jnp.broadcast_to(dest, dest_ref.shape)
    wide = (iota((n, 8 * n), 1) & (n - 1)) == iota((n, 8 * n), 0)
    dest_wide = jnp.sum(jnp.where(wide, dest, 0.0), 0, keepdims=True).astype(I32)
    dest_row = dest_wide[:, :n]
    i = iota((CHUNK * n, 1), 0)
    chunk = (i * 3641) >> 16
    rest = i - CHUNK * chunk
    place, part = chunk * 2 + (rest & 1), rest >> 1
    where_from = iota((1, 8 * n), 1)
    pick = onehot((place == dest_wide) & (part == (where_from >> 5)))
    pick_slot = onehot((place == dest_row) & (part == 8))
    slots = jnp.broadcast_to(slot, (n, HD)).astype(BF)
    sent = mm(pick_slot, slots)
    copies[2].wait()
    send_ref[...] = (sent + mm(pick, chunked(hidden_ref[...]))).astype(BF)


def down_body(recv_ref, down_at, part_ref, slot_ref, down_ref, wide_ref, sems):
    count = down_at.shape[0]
    parts = sems.shape[0]
    each = count // parts
    pieces = [slice(k * each, (k + 1) * each) for k in range(parts)]
    copies = fetch([down_at.at[p] for p in pieces], [down_ref.at[p] for p in pieces], sems)
    n = recv_ref.shape[0] // CHUNK
    m = 2 * n
    wide_ref[...] = recv_ref[...].astype(F32)
    rows = wide_ref[...].reshape(n, CHUNK, HD)
    x = [rows[:, 2 * c : 2 * c + 2, :].reshape(m, HD).astype(BF) for c in range(CHUNK // 2 - 1)]
    x = jnp.concatenate(x, 1)
    slot = rows[:, CHUNK - 2 :, :].reshape(m, HD)
    slot_ref[...] = slot
    total = jnp.zeros((m, HD), F32)
    for a in range(0, count, 2):
        if a % each == 0:
            copies[a // each].wait()
        y = mm(x, jnp.concatenate([down_ref[a], down_ref[a + 1]], 1))
        total = total + jnp.where(slot == a, y[:, :HD], 0.0)
        total = total + jnp.where(slot == a + 1, y[:, HD:], 0.0)
    part_ref[...] = total


def up_body(p0_ref, p1_ref, p2_ref, p3_ref, slot_ref, up_ref, send_ref):
    m = slot_ref.shape[0]
    down = (p0_ref[...] + p1_ref[...]) + (p2_ref[...] + p3_ref[...])
    first = iota((m, HD), 1) < HD // 2
    both = jnp.concatenate([jnp.where(first, down, 0.0), jnp.where(first, 0.0, down)], 0)
    slot = jnp.concatenate([slot_ref[...]] * 2, 0)
    count = up_ref.shape[0] // HD
    picked = jnp.concatenate(
        [jnp.where(slot == a, both, 0.0).astype(BF) for a in range(count)], 1
    )
    lora = mm(picked, up_ref[...])
    i, j = iota((2 * m, 1), 0), iota((1, 2 * m), 1)
    order = onehot((i & 1) * m + (i >> 1) == j)
    send_ref[...] = mm(order, lora.astype(BF)).astype(BF)


def attend_cached(q_ref, pages_ref, tables_ref, lengths_ref, cache_ref):
    n = q_ref.shape[0]
    heads = q_ref.shape[1] // HD
    page = HD
    count = pages_ref.shape[0] // (2 * page)
    tokens = count * page
    eye = onehot(iota((n, n), 0) == iota((n, n), 1))
    tables = mm_t(eye, tables_ref[...].astype(F32).astype(BF)).astype(I32)
    length = column(lengths_ref[...].astype(F32), n).astype(I32)
    at = iota((n, tokens), 1)
    page_id, place = at >> 7, at & (page - 1)
    counts = jnp.zeros((n, tokens), F32)
    for j in range(tables_ref.shape[0]):
        hit = (tables[:, j : j + 1] == page_id) & (place < length - j * page)
        counts = counts + jnp.where(hit, 1.0, 0.0)
    i, j = iota((2 * page, 2 * page), 0), iota((2 * page, 2 * page), 1)
    part = onehot((i & (page - 1)) * 2 + (i >> 7) == j)
    keys, values = [], []
    for p in range(count):
        both = mm(part, pages_ref[p * 2 * page : (p + 1) * 2 * page, :]).astype(BF)
        keys.append(both[:page])
        values.append(both[page:])
    keys = jnp.concatenate(keys, 0)
    values = jnp.concatenate(values, 0)
    for h in range(heads):
        scores = mm_t(q_ref[:, h * HD : (h + 1) * HD], keys) * (1.0 / math.sqrt(HD))
        scores = jnp.where(counts > 0.0, scores, -jnp.inf)
        top = jnp.max(scores, 1, keepdims=True)
        weights = jnp.exp(scores - top) * counts
        rows = slice(h * n, (h + 1) * n)
        cache_ref[0, rows, :] = mm(weights.astype(BF), values)
        cache_ref[1, rows, :] = jnp.broadcast_to(top, (n, HD))
        cache_ref[2, rows, :] = jnp.broadcast_to(jnp.sum(weights, 1, keepdims=True), (n, HD))


def widened(x):
    n = x.shape[0]
    chunks = x.shape[1] // HD
    i, j = iota((HD, 4 * HD), 0), iota((HD, 4 * HD), 1)
    e = mm(chunked(x), onehot((j & 255) == 2 * i + (j >> 8))).astype(BF)
    parts = [
        jnp.concatenate([e[g * n : (g + 1) * n, c * 256 : (c + 1) * 256] for g in range(chunks)], 1)
        for c in range(2)
    ]
    return jnp.concatenate(parts, 0)


def widen_body(x_ref, own_ref):
    own_ref[...] = widened(x_ref[...])


def wait_body(
    index_ref,
    own_ref,
    mine_ref,
    other_ref,
    q_ref,
    pages_ref,
    tables_ref,
    lengths_ref,
    w_at,
    base_ref,
    cache_ref,
    w_ref,
    sems,
):
    me = index_ref[0]
    _, n, width = mine_ref.shape
    away = [(dy, dc) for dy in range(4) for dc in range(2)]
    spots = []
    for dy, dc in away:
        peer = (((me >> 1) + 4 - dy) & 3) * 2 + ((me & 1) ^ dc)
        spots.append(pl.ds(pl.multiple_of(peer * (2 * width), 2 * width), 2 * width))
    copies = fetch([w_at.at[p] for p in spots], [w_ref.at[k] for k in range(8)], sems)
    attend_cached(q_ref, pages_ref, tables_ref, lengths_ref, cache_ref)
    total = jnp.zeros((2 * n, HD), F32)
    for k, (dy, dc) in enumerate(away):
        both = own_ref[...] if k == 0 else widened((mine_ref, other_ref)[dc][dy])
        copies[k].wait()
        total = total + mm(both, w_ref[k])
    base_ref[...] = total


def finish_body(
    recv_ref, dest_ref, base_ref, cos_ref, sin_ref, q_ref, cache_ref, att_ref, new_ref
):
    n = q_ref.shape[0]
    heads = q_ref.shape[1] // HD
    dest = dest_ref[...].astype(I32)
    dest = jnp.concatenate([dest, dest], 0)
    i, j = iota((2 * n, 1), 0), iota((1, 4 * n), 1)
    back = onehot((dest == (j >> 1)) & ((j & 1) == (i >> 5)))
    lora = mm(back, recv_ref[...])
    combined = base_ref[...] + ADAPTER_SCALE * lora
    key = combined[:n]
    half = HD // 2
    turned = jnp.concatenate([key[:, half:], key[:, :half]], 1)
    key = key * cos_ref[...] + turned * sin_ref[...]
    new = jnp.concatenate([key, combined[n:]], 0).astype(BF)
    i, j = iota((2 * n, 2 * n), 0), iota((2 * n, 2 * n), 1)
    new_ref[...] = mm(onehot((i & 1) * n + (i >> 1) == j), new).astype(BF)
    key = new[:n].astype(F32)
    value = new[n:].astype(F32)
    for h in range(heads):
        rows = slice(h * n, (h + 1) * n)
        q = q_ref[:, h * HD : (h + 1) * HD].astype(F32)
        own = jnp.sum(q * key, 1, keepdims=True) * (1.0 / math.sqrt(HD))
        top = cache_ref[1, rows, :]
        high = jnp.maximum(top, own)
        old = jnp.exp(top - high)
        mine = jnp.exp(own - high)
        mixed = cache_ref[0, rows, :] * old + mine * value
        att_ref[:, h * HD : (h + 1) * HD] = (mixed / (cache_ref[2, rows, :] * old + mine)).astype(BF)


def shape(dims, dtype):
    return jax.ShapeDtypeStruct(dims, dtype)


def per_device(
    hidden, queries, w_kv, adapters_down, adapters_up, kv_pages, tenant_ids, owner_table, page_tables, lengths
):
    n = hidden.shape[0]
    width = hidden.shape[1]

    def swap_core(a):
        return lax.ppermute(a, "tp", [(i, i ^ 1) for i in range(8)])

    def along_y(a):
        return [
            lax.ppermute(a, "tp", [(i, ((i // 2 + d) % 4) * 2 + i % 2) for i in range(8)])
            for d in (1, 2, 3)
        ]

    entries = owner_table.shape[0]
    send, dest = call(
        route_body,
        (shape((n * CHUNK, HD), BF), shape((n, HD), F32)),
        3,
        2 * 576 * 256 * 128,
        300000,
        scratch=(
            pltpu.VMEM((n, width), BF),
            pltpu.VMEM((1, n), I32),
            pltpu.VMEM((1, entries), I32),
            pltpu.SemaphoreType.DMA((3,)),
        ),
        limit=ALL,
        far=(0, 1, 2),
    )(hidden, tenant_ids.reshape(1, -1), owner_table.reshape(1, -1))
    send = send.reshape(n, CHUNK // 2, 2, HD)
    recv = lax.all_to_all(send, "pool", 0, 0, tiled=True).reshape(n * CHUNK, HD)

    _, tied = lax.optimization_barrier((send, hidden))
    far = along_y(tied)
    own = call(widen_body, shape((2 * n, 2 * width), BF), 1, 2 * 512 * 256 * 128, 8000000)(hidden)
    recv, own, *far = lax.optimization_barrier((recv, own, *far))

    part, slot = call(
        down_body,
        (shape((2 * n, HD), F32), shape((2 * n, HD), F32)),
        2,
        2 * 64 * 16 * 1024 * 128,
        4500000,
        scratch=(
            pltpu.VMEM(adapters_down.shape, BF),
            pltpu.VMEM((n * CHUNK, HD), F32),
            pltpu.SemaphoreType.DMA((2,)),
        ),
        limit=MOST,
        far=(1,),
    )(recv, adapters_down)
    part = part + swap_core(part)
    part, *far = lax.optimization_barrier((part, *far))
    sums = along_y(part)
    mine = jnp.stack([hidden, *far])
    half = HD // 2
    frequency = 10000.0 ** (-jnp.arange(half, dtype=F32) * 2.0 / HD)
    angles = lengths.astype(F32)[:, None] * frequency
    cosine, sine = jnp.cos(angles), jnp.sin(angles)
    cosine = jnp.concatenate([cosine, cosine], 1)
    sine = jnp.concatenate([-sine, sine], 1)
    mine, cosine, sine, *sums = lax.optimization_barrier((mine, cosine, sine, *sums))
    back = call(up_body, shape((4 * n, HD), BF), 6, 2 * 128 * 2048 * 128, 600000)(
        part, *sums, slot, adapters_up.reshape(-1, HD)
    )
    sent = back.reshape(n, 2, 2, HD)
    result = lax.all_to_all(sent, "pool", 0, 0, tiled=True).reshape(4 * n, HD)
    _, mine = lax.optimization_barrier((back, mine))
    other = swap_core(mine)

    pages = kv_pages.reshape(-1, HD)
    me = lax.axis_index("tp").astype(I32).reshape(1)
    base, cache = call(
        wait_body,
        (shape((2 * n, HD), F32), shape((3, 8 * n, HD), F32)),
        9,
        4 * 64 * 8192 * 128 + 4 * 256 * 1024 * 128,
        16000000,
        scratch=(
            pltpu.VMEM((8, 2 * width, HD), BF),
            pltpu.SemaphoreType.DMA((8,)),
        ),
        limit=MOST,
        smem=(0,),
        far=(8,),
    )(
        me,
        own,
        mine,
        other,
        queries,
        pages,
        page_tables.T,
        lengths.reshape(1, -1),
        w_kv.reshape(-1, HD),
    )

    attention, new_kv = call(
        finish_body, (shape((n, width), BF), shape((2 * n, HD), BF)), 7, 1000000, 1000000
    )(result, dest, base, cosine, sine, queries, cache)
    return attention, new_kv.reshape(n, 2, HD)


def solution(mesh):
    in_specs = (
        P("pool", "tp"),
        P("pool", "tp"),
        P(None, None, "tp"),
        P("pool", "tp", None),
        P("pool", None, None, "tp"),
        P("pool", None, None, "tp"),
        P("pool"),
        P(),
        P("pool", None),
        P("pool"),
    )
    out_specs = (P("pool", "tp"), P("pool", None, "tp"))
    return jax.shard_map(
        per_device, mesh=mesh, in_specs=in_specs, out_specs=out_specs, check_vma=False
    )
```

```python
import math

import jax
import jax.numpy as jnp
from jax import lax
from jax.experimental import pallas as pl
from jax.experimental.pallas import tpu as pltpu
from jax.sharding import PartitionSpec as P

HD = 128
ADAPTER_SCALE = 0.5
BF = jnp.bfloat16
F32 = jnp.float32
I32 = jnp.int32
VMEM = pl.BlockSpec(memory_space=pltpu.VMEM)
SMEM = pl.BlockSpec(memory_space=pltpu.SMEM)
HBM = pl.BlockSpec(memory_space=pl.ANY)
ALL = 58
MOST = 52
CHUNK = 18


def iota(shape, dim):
    return lax.broadcasted_iota(I32, shape, dim)


def mm(a, b):
    return jnp.dot(a, b, preferred_element_type=F32)


def mm_t(a, b):
    return lax.dot_general(a, b, (((1,), (1,)), ((), ())), preferred_element_type=F32)


def onehot(mask):
    return jnp.where(mask, 1.0, 0.0).astype(BF)


def column(row, n):
    return jnp.sum(jnp.where(iota((n, n), 0) == iota((n, n), 1), row, 0.0), 1, keepdims=True)


def chunked(x):
    return jnp.concatenate([x[:, i * HD : (i + 1) * HD] for i in range(x.shape[1] // HD)], 0)


def call(body, outs, n_in, flops=0, read=0, scratch=(), limit=16, smem=(), far=()):
    return pl.pallas_call(
        body,
        out_shape=outs,
        in_specs=[SMEM if i in smem else HBM if i in far else VMEM for i in range(n_in)],
        out_specs=jax.tree.map(lambda _: VMEM, outs),
        scratch_shapes=scratch,
        compiler_params=pltpu.CompilerParams(vmem_limit_bytes=limit << 20),
        cost_estimate=pl.CostEstimate(flops=flops, bytes_accessed=read, transcendentals=0),
    )


def fetch(sources, targets, sems):
    copies = [
        pltpu.make_async_copy(source, target, sems.at[i])
        for i, (source, target) in enumerate(zip(sources, targets))
    ]
    for copy in copies:
        copy.start()
    return copies


def route_body(
    hidden_at, tenants_at, table_at, send_ref, dest_ref, hidden_ref, tenants_ref, table_ref, sems
):
    copies = fetch(
        (tenants_at, table_at, hidden_at), (tenants_ref, table_ref, hidden_ref), sems
    )
    copies[0].wait()
    copies[1].wait()
    n = tenants_ref.shape[1]
    tenant = column(tenants_ref[...].astype(F32), n)
    entries = table_ref.shape[1]
    table = table_ref[...].astype(F32)
    lanes = iota((n, entries), 1).astype(F32)
    storage = jnp.sum(jnp.where(tenant == lanes, table, 0.0), 1, keepdims=True).astype(I32)
    owner = (storage >> 4).astype(F32)
    slot = (storage & 15).astype(F32)
    eye = iota((n, n), 0) == iota((n, n), 1)
    owner_row = jnp.sum(jnp.where(eye, owner, 0.0), 0, keepdims=True)
    same = (owner == owner_row) & (iota((n, n), 1) < iota((n, n), 0))
    rank = jnp.sum(jnp.where(same, 1.0, 0.0), 1, keepdims=True)
    dest = owner * 2.0 + rank
    dest_ref[...] = jnp.broadcast_to(dest, dest_ref.shape)
    wide = (iota((n, 8 * n), 1) & (n - 1)) == iota((n, 8 * n), 0)
    dest_wide = jnp.sum(jnp.where(wide, dest, 0.0), 0, keepdims=True).astype(I32)
    dest_row = dest_wide[:, :n]
    i = iota((CHUNK * n, 1), 0)
    chunk = (i * 3641) >> 16
    rest = i - CHUNK * chunk
    place, part = chunk * 2 + (rest & 1), rest >> 1
    where_from = iota((1, 8 * n), 1)
    pick = onehot((place == dest_wide) & (part == (where_from >> 5)))
    pick_slot = onehot((place == dest_row) & (part == 8))
    slots = jnp.broadcast_to(slot, (n, HD)).astype(BF)
    sent = mm(pick_slot, slots)
    copies[2].wait()
    send_ref[...] = (sent + mm(pick, chunked(hidden_ref[...]))).astype(BF)


def down_body(recv_ref, down_at, part_ref, slot_ref, down_ref, wide_ref, sems):
    count = down_at.shape[0]
    parts = sems.shape[0]
    each = count // parts
    pieces = [slice(k * each, (k + 1) * each) for k in range(parts)]
    copies = fetch([down_at.at[p] for p in pieces], [down_ref.at[p] for p in pieces], sems)
    n = recv_ref.shape[0] // CHUNK
    m = 2 * n
    wide_ref[...] = recv_ref[...].astype(F32)
    rows = wide_ref[...].reshape(n, CHUNK, HD)
    x = [rows[:, 2 * c : 2 * c + 2, :].reshape(m, HD).astype(BF) for c in range(CHUNK // 2 - 1)]
    x = jnp.concatenate(x, 1)
    slot = rows[:, CHUNK - 2 :, :].reshape(m, HD)
    slot_ref[...] = slot
    total = jnp.zeros((m, HD), F32)
    for a in range(0, count, 2):
        if a % each == 0:
            copies[a // each].wait()
        y = mm(x, jnp.concatenate([down_ref[a], down_ref[a + 1]], 1))
        total = total + jnp.where(slot == a, y[:, :HD], 0.0)
        total = total + jnp.where(slot == a + 1, y[:, HD:], 0.0)
    part_ref[...] = total


def up_body(p0_ref, p1_ref, p2_ref, p3_ref, slot_ref, up_ref, send_ref):
    m = slot_ref.shape[0]
    down = (p0_ref[...] + p1_ref[...]) + (p2_ref[...] + p3_ref[...])
    first = iota((m, HD), 1) < HD // 2
    both = jnp.concatenate([jnp.where(first, down, 0.0), jnp.where(first, 0.0, down)], 0)
    slot = jnp.concatenate([slot_ref[...]] * 2, 0)
    count = up_ref.shape[0] // HD
    picked = jnp.concatenate(
        [jnp.where(slot == a, both, 0.0).astype(BF) for a in range(count)], 1
    )
    lora = mm(picked, up_ref[...])
    i, j = iota((2 * m, 1), 0), iota((1, 2 * m), 1)
    order = onehot((i & 1) * m + (i >> 1) == j)
    send_ref[...] = mm(order, lora.astype(BF)).astype(BF)


def attend_cached(q_ref, pages_ref, tables_ref, lengths_ref, cache_ref):
    n = q_ref.shape[0]
    heads = q_ref.shape[1] // HD
    page = HD
    count = pages_ref.shape[0] // (2 * page)
    tokens = count * page
    eye = onehot(iota((n, n), 0) == iota((n, n), 1))
    tables = mm_t(eye, tables_ref[...].astype(F32).astype(BF)).astype(I32)
    length = column(lengths_ref[...].astype(F32), n).astype(I32)
    at = iota((n, tokens), 1)
    page_id, place = at >> 7, at & (page - 1)
    counts = jnp.zeros((n, tokens), F32)
    for j in range(tables_ref.shape[0]):
        hit = (tables[:, j : j + 1] == page_id) & (place < length - j * page)
        counts = counts + jnp.where(hit, 1.0, 0.0)
    i, j = iota((2 * page, 2 * page), 0), iota((2 * page, 2 * page), 1)
    part = onehot((i & (page - 1)) * 2 + (i >> 7) == j)
    keys, values = [], []
    for p in range(count):
        both = mm(part, pages_ref[p * 2 * page : (p + 1) * 2 * page, :]).astype(BF)
        keys.append(both[:page])
        values.append(both[page:])
    keys = jnp.concatenate(keys, 0)
    values = jnp.concatenate(values, 0)
    for h in range(heads):
        scores = mm_t(q_ref[:, h * HD : (h + 1) * HD], keys) * (1.0 / math.sqrt(HD))
        scores = jnp.where(counts > 0.0, scores, -jnp.inf)
        top = jnp.max(scores, 1, keepdims=True)
        weights = jnp.exp(scores - top) * counts
        rows = slice(h * n, (h + 1) * n)
        cache_ref[0, rows, :] = mm(weights.astype(BF), values)
        cache_ref[1, rows, :] = jnp.broadcast_to(top, (n, HD))
        cache_ref[2, rows, :] = jnp.broadcast_to(jnp.sum(weights, 1, keepdims=True), (n, HD))


def widened(x):
    n = x.shape[0]
    chunks = x.shape[1] // HD
    i, j = iota((HD, 4 * HD), 0), iota((HD, 4 * HD), 1)
    e = mm(chunked(x), onehot((j & 255) == 2 * i + (j >> 8))).astype(BF)
    parts = [
        jnp.concatenate([e[g * n : (g + 1) * n, c * 256 : (c + 1) * 256] for g in range(chunks)], 1)
        for c in range(2)
    ]
    return jnp.concatenate(parts, 0)


def widen_body(x_ref, own_ref):
    own_ref[...] = widened(x_ref[...])


def fetch_rows(flips, index_ref, n, width, w_at, w_ref, sems):
    me = index_ref[0]
    spots = []
    for flip in flips:
        for dc in range(2):
            peer = ((me >> 1) ^ flip) * 2 + ((me & 1) ^ dc)
            spots.append(pl.ds(pl.multiple_of(peer * (2 * width), 2 * width), 2 * width))
    steps = range(len(spots))
    return fetch([w_at.at[p] for p in spots], [w_ref.at[k] for k in steps], sems)


def project(widened_rows, w_ref, copies):
    total = 0.0
    for k, copy in enumerate(copies):
        both = widened_rows(k)
        copy.wait()
        total = total + mm(both, w_ref[k])
    return total


def wait_body(
    index_ref,
    own_ref,
    mine_ref,
    across_ref,
    diagonal_ref,
    q_ref,
    pages_ref,
    tables_ref,
    lengths_ref,
    w_at,
    base_ref,
    cache_ref,
    w_ref,
    sems,
):
    _, n, width = mine_ref.shape
    copies = fetch_rows((0, 1), index_ref, n, width, w_at, w_ref, sems)
    attend_cached(q_ref, pages_ref, tables_ref, lengths_ref, cache_ref)
    rows = (
        lambda: own_ref[...],
        lambda: widened(across_ref[...]),
        lambda: widened(mine_ref[1]),
        lambda: widened(diagonal_ref[...]),
    )
    base_ref[...] = project(lambda k: rows[k](), w_ref, copies)


def far_body(index_ref, mine_ref, other_ref, w_at, base_ref, w_ref, sems):
    _, n, width = mine_ref.shape
    copies = fetch_rows((3, 2), index_ref, n, width, w_at, w_ref, sems)
    base_ref[...] = project(
        lambda k: widened((mine_ref, other_ref)[k & 1][k >> 1]), w_ref, copies
    )


def finish_body(
    recv_ref, dest_ref, near_ref, far_ref, cos_ref, sin_ref, q_ref, cache_ref, att_ref, new_ref
):
    n = q_ref.shape[0]
    heads = q_ref.shape[1] // HD
    dest = dest_ref[...].astype(I32)
    dest = jnp.concatenate([dest, dest], 0)
    i, j = iota((2 * n, 1), 0), iota((1, 4 * n), 1)
    back = onehot((dest == (j >> 1)) & ((j & 1) == (i >> 5)))
    lora = mm(back, recv_ref[...])
    combined = near_ref[...] + far_ref[...] + ADAPTER_SCALE * lora
    key = combined[:n]
    half = HD // 2
    turned = jnp.concatenate([key[:, half:], key[:, :half]], 1)
    key = key * cos_ref[...] + turned * sin_ref[...]
    new = jnp.concatenate([key, combined[n:]], 0).astype(BF)
    i, j = iota((2 * n, 2 * n), 0), iota((2 * n, 2 * n), 1)
    new_ref[...] = mm(onehot((i & 1) * n + (i >> 1) == j), new).astype(BF)
    key = new[:n].astype(F32)
    value = new[n:].astype(F32)
    for h in range(heads):
        rows = slice(h * n, (h + 1) * n)
        q = q_ref[:, h * HD : (h + 1) * HD].astype(F32)
        own = jnp.sum(q * key, 1, keepdims=True) * (1.0 / math.sqrt(HD))
        top = cache_ref[1, rows, :]
        high = jnp.maximum(top, own)
        old = jnp.exp(top - high)
        mine = jnp.exp(own - high)
        mixed = cache_ref[0, rows, :] * old + mine * value
        att_ref[:, h * HD : (h + 1) * HD] = (mixed / (cache_ref[2, rows, :] * old + mine)).astype(BF)


def shape(dims, dtype):
    return jax.ShapeDtypeStruct(dims, dtype)


def per_device(
    hidden, queries, w_kv, adapters_down, adapters_up, kv_pages, tenant_ids, owner_table, page_tables, lengths
):
    n = hidden.shape[0]
    width = hidden.shape[1]

    def swap(a, flip):
        return lax.ppermute(a, "tp", [(i, i ^ flip) for i in range(8)])

    def along_y(a):
        return [
            lax.ppermute(a, "tp", [(i, ((i // 2 + d) % 4) * 2 + i % 2) for i in range(8)])
            for d in (1, 2, 3)
        ]

    entries = owner_table.shape[0]
    send, dest = call(
        route_body,
        (shape((n * CHUNK, HD), BF), shape((n, HD), F32)),
        3,
        2 * 576 * 256 * 128,
        300000,
        scratch=(
            pltpu.VMEM((n, width), BF),
            pltpu.VMEM((1, n), I32),
            pltpu.VMEM((1, entries), I32),
            pltpu.SemaphoreType.DMA((3,)),
        ),
        limit=ALL,
        far=(0, 1, 2),
    )(hidden, tenant_ids.reshape(1, -1), owner_table.reshape(1, -1))
    send = send.reshape(n, CHUNK // 2, 2, HD)
    recv = lax.all_to_all(send, "pool", 0, 0, tiled=True).reshape(n * CHUNK, HD)

    _, tied = lax.optimization_barrier((send, hidden))
    beside, across, diagonal = swap(tied, 2), swap(tied, 1), swap(tied, 3)
    own = call(widen_body, shape((2 * n, 2 * width), BF), 1, 2 * 512 * 256 * 128, 8000000)(hidden)
    near = jnp.stack([hidden, beside])
    recv, own, near, across, diagonal = lax.optimization_barrier((recv, own, near, across, diagonal))

    part, slot = call(
        down_body,
        (shape((2 * n, HD), F32), shape((2 * n, HD), F32)),
        2,
        2 * 64 * 16 * 1024 * 128,
        4500000,
        scratch=(
            pltpu.VMEM(adapters_down.shape, BF),
            pltpu.VMEM((n * CHUNK, HD), F32),
            pltpu.SemaphoreType.DMA((2,)),
        ),
        limit=MOST,
        far=(1,),
    )(recv, adapters_down)
    part = part + swap(part, 1)
    sums = along_y(part)
    _, tied = lax.optimization_barrier((part, near))
    far, far_across = swap(tied, 6), swap(tied, 7)
    half = HD // 2
    frequency = 10000.0 ** (-jnp.arange(half, dtype=F32) * 2.0 / HD)
    angles = lengths.astype(F32)[:, None] * frequency
    cosine, sine = jnp.cos(angles), jnp.sin(angles)
    cosine = jnp.concatenate([cosine, cosine], 1)
    sine = jnp.concatenate([-sine, sine], 1)
    cosine, sine, *sums = lax.optimization_barrier((cosine, sine, *sums))
    back = call(up_body, shape((4 * n, HD), BF), 6, 2 * 128 * 2048 * 128, 600000)(
        part, *sums, slot, adapters_up.reshape(-1, HD)
    )
    sent = back.reshape(n, 2, 2, HD)
    result = lax.all_to_all(sent, "pool", 0, 0, tiled=True).reshape(4 * n, HD)
    _, queries = lax.optimization_barrier((back, queries))

    pages = kv_pages.reshape(-1, HD)
    me = lax.axis_index("tp").astype(I32).reshape(1)
    base, cache = call(
        wait_body,
        (shape((2 * n, HD), F32), shape((3, 8 * n, HD), F32)),
        10,
        4 * 64 * 8192 * 128 + 4 * 256 * 1024 * 128,
        16000000,
        scratch=(
            pltpu.VMEM((4, 2 * width, HD), BF),
            pltpu.SemaphoreType.DMA((4,)),
        ),
        limit=MOST,
        smem=(0,),
        far=(9,),
    )(
        me,
        own,
        near,
        across,
        diagonal,
        queries,
        pages,
        page_tables.T,
        lengths.reshape(1, -1),
        w_kv.reshape(-1, HD),
    )

    rest = call(
        far_body,
        shape((2 * n, HD), F32),
        4,
        0,
        1000,
        scratch=(pltpu.VMEM((4, 2 * width, HD), BF), pltpu.SemaphoreType.DMA((4,))),
        limit=MOST,
        smem=(0,),
        far=(3,),
    )(me, far, far_across, w_kv.reshape(-1, HD))

    attention, new_kv = call(
        finish_body, (shape((n, width), BF), shape((2 * n, HD), BF)), 8, 1000000, 1000000
    )(result, dest, base, rest, cosine, sine, queries, cache)
    return attention, new_kv.reshape(n, 2, HD)


def solution(mesh):
    in_specs = (
        P("pool", "tp"),
        P("pool", "tp"),
        P(None, None, "tp"),
        P("pool", "tp", None),
        P("pool", None, None, "tp"),
        P("pool", None, None, "tp"),
        P("pool"),
        P(),
        P("pool", None),
        P("pool"),
    )
    out_specs = (P("pool", "tp"), P("pool", None, "tp"))
    return jax.shard_map(
        per_device, mesh=mesh, in_specs=in_specs, out_specs=out_specs, check_vma=False
    )
```

```python
import math

import jax
import jax.numpy as jnp
from jax import lax
from jax.experimental import pallas as pl
from jax.experimental.pallas import tpu as pltpu
from jax.sharding import PartitionSpec as P

HD = 128
ADAPTER_SCALE = 0.5
BF = jnp.bfloat16
F32 = jnp.float32
I32 = jnp.int32
VMEM = pl.BlockSpec(memory_space=pltpu.VMEM)
SMEM = pl.BlockSpec(memory_space=pltpu.SMEM)
HBM = pl.BlockSpec(memory_space=pl.ANY)
ALL = 58
MOST = 52
SOME = 50
EARLY = 6
CHUNK = 18


def iota(shape, dim):
    return lax.broadcasted_iota(I32, shape, dim)


def mm(a, b):
    return jnp.dot(a, b, preferred_element_type=F32)


def mm_t(a, b):
    return lax.dot_general(a, b, (((1,), (1,)), ((), ())), preferred_element_type=F32)


def onehot(mask):
    return jnp.where(mask, 1.0, 0.0).astype(BF)


def column(row, n):
    return jnp.sum(jnp.where(iota((n, n), 0) == iota((n, n), 1), row, 0.0), 1, keepdims=True)


def chunked(x):
    return jnp.concatenate([x[:, i * HD : (i + 1) * HD] for i in range(x.shape[1] // HD)], 0)


def call(body, outs, n_in, flops=0, read=0, scratch=(), limit=16, smem=(), far=()):
    return pl.pallas_call(
        body,
        out_shape=outs,
        in_specs=[SMEM if i in smem else HBM if i in far else VMEM for i in range(n_in)],
        out_specs=jax.tree.map(lambda _: VMEM, outs),
        scratch_shapes=scratch,
        compiler_params=pltpu.CompilerParams(vmem_limit_bytes=limit << 20),
        cost_estimate=pl.CostEstimate(flops=flops, bytes_accessed=read, transcendentals=0),
    )


def fetch(sources, targets, sems):
    copies = [
        pltpu.make_async_copy(source, target, sems.at[i])
        for i, (source, target) in enumerate(zip(sources, targets))
    ]
    for copy in copies:
        copy.start()
    return copies


def route_body(
    hidden_at, tenants_at, table_at, send_ref, dest_ref, hidden_ref, tenants_ref, table_ref, sems
):
    copies = fetch(
        (tenants_at, table_at, hidden_at), (tenants_ref, table_ref, hidden_ref), sems
    )
    copies[0].wait()
    copies[1].wait()
    n = tenants_ref.shape[1]
    tenant = column(tenants_ref[...].astype(F32), n)
    entries = table_ref.shape[1]
    table = table_ref[...].astype(F32)
    lanes = iota((n, entries), 1).astype(F32)
    storage = jnp.sum(jnp.where(tenant == lanes, table, 0.0), 1, keepdims=True).astype(I32)
    owner = (storage >> 4).astype(F32)
    slot = (storage & 15).astype(F32)
    eye = iota((n, n), 0) == iota((n, n), 1)
    owner_row = jnp.sum(jnp.where(eye, owner, 0.0), 0, keepdims=True)
    same = (owner == owner_row) & (iota((n, n), 1) < iota((n, n), 0))
    rank = jnp.sum(jnp.where(same, 1.0, 0.0), 1, keepdims=True)
    dest = owner * 2.0 + rank
    dest_ref[...] = jnp.broadcast_to(dest, dest_ref.shape)
    wide = (iota((n, 8 * n), 1) & (n - 1)) == iota((n, 8 * n), 0)
    dest_wide = jnp.sum(jnp.where(wide, dest, 0.0), 0, keepdims=True).astype(I32)
    dest_row = dest_wide[:, :n]
    i = iota((CHUNK * n, 1), 0)
    chunk = (i * 3641) >> 16
    rest = i - CHUNK * chunk
    place, part = chunk * 2 + (rest & 1), rest >> 1
    where_from = iota((1, 8 * n), 1)
    pick = onehot((place == dest_wide) & (part == (where_from >> 5)))
    pick_slot = onehot((place == dest_row) & (part == 8))
    slots = jnp.broadcast_to(slot, (n, HD)).astype(BF)
    sent = mm(pick_slot, slots)
    copies[2].wait()
    send_ref[...] = (sent + mm(pick, chunked(hidden_ref[...]))).astype(BF)


def early_body(down_at, first_ref, sems):
    (copy,) = fetch([down_at.at[: first_ref.shape[0]]], [first_ref], sems)
    copy.wait()


def down_body(
    recv_ref, first_ref, near_ref, beside_ref, down_at, part_ref, slot_ref, pair_ref, down_ref, wide_ref, sems
):
    early = first_ref.shape[0]
    (copy,) = fetch([down_at.at[early:]], [down_ref], sems)
    pair_ref[0] = near_ref[...]
    pair_ref[1] = beside_ref[...]
    n = recv_ref.shape[0] // CHUNK
    m = 2 * n
    wide_ref[...] = recv_ref[...].astype(F32)
    rows = wide_ref[...].reshape(n, CHUNK, HD)
    x = [rows[:, 2 * c : 2 * c + 2, :].reshape(m, HD).astype(BF) for c in range(CHUNK // 2 - 1)]
    x = jnp.concatenate(x, 1)
    slot = rows[:, CHUNK - 2 :, :].reshape(m, HD)
    slot_ref[...] = slot
    total = jnp.zeros((m, HD), F32)
    for a in range(0, down_at.shape[0], 2):
        if a < early:
            two = first_ref[a], first_ref[a + 1]
        else:
            if a == early:
                copy.wait()
            two = down_ref[a - early], down_ref[a - early + 1]
        y = mm(x, jnp.concatenate(two, 1))
        total = total + jnp.where(slot == a, y[:, :HD], 0.0)
        total = total + jnp.where(slot == a + 1, y[:, HD:], 0.0)
    part_ref[...] = total


def up_body(p0_ref, p1_ref, p2_ref, p3_ref, slot_ref, up_ref, send_ref):
    m = slot_ref.shape[0]
    down = (p0_ref[...] + p1_ref[...]) + (p2_ref[...] + p3_ref[...])
    first = iota((m, HD), 1) < HD // 2
    both = jnp.concatenate([jnp.where(first, down, 0.0), jnp.where(first, 0.0, down)], 0)
    slot = jnp.concatenate([slot_ref[...]] * 2, 0)
    count = up_ref.shape[0] // HD
    picked = jnp.concatenate(
        [jnp.where(slot == a, both, 0.0).astype(BF) for a in range(count)], 1
    )
    lora = mm(picked, up_ref[...])
    i, j = iota((2 * m, 1), 0), iota((1, 2 * m), 1)
    order = onehot((i & 1) * m + (i >> 1) == j)
    send_ref[...] = mm(order, lora.astype(BF)).astype(BF)


def attend_cached(q_ref, pages_ref, tables_ref, lengths_ref, cache_ref):
    n = q_ref.shape[0]
    heads = q_ref.shape[1] // HD
    page = HD
    count = pages_ref.shape[0] // (2 * page)
    tokens = count * page
    eye = onehot(iota((n, n), 0) == iota((n, n), 1))
    tables = mm_t(eye, tables_ref[...].astype(F32).astype(BF)).astype(I32)
    length = column(lengths_ref[...].astype(F32), n).astype(I32)
    at = iota((n, tokens), 1)
    page_id, place = at >> 7, at & (page - 1)
    counts = jnp.zeros((n, tokens), F32)
    for j in range(tables_ref.shape[0]):
        hit = (tables[:, j : j + 1] == page_id) & (place < length - j * page)
        counts = counts + jnp.where(hit, 1.0, 0.0)
    i, j = iota((2 * page, 2 * page), 0), iota((2 * page, 2 * page), 1)
    part = onehot((i & (page - 1)) * 2 + (i >> 7) == j)
    keys, values = [], []
    for p in range(count):
        both = mm(part, pages_ref[p * 2 * page : (p + 1) * 2 * page, :]).astype(BF)
        keys.append(both[:page])
        values.append(both[page:])
    keys = jnp.concatenate(keys, 0)
    values = jnp.concatenate(values, 0)
    for h in range(heads):
        scores = mm_t(q_ref[:, h * HD : (h + 1) * HD], keys) * (1.0 / math.sqrt(HD))
        scores = jnp.where(counts > 0.0, scores, -jnp.inf)
        top = jnp.max(scores, 1, keepdims=True)
        weights = jnp.exp(scores - top) * counts
        rows = slice(h * n, (h + 1) * n)
        cache_ref[0, rows, :] = mm(weights.astype(BF), values)
        cache_ref[1, rows, :] = jnp.broadcast_to(top, (n, HD))
        cache_ref[2, rows, :] = jnp.broadcast_to(jnp.sum(weights, 1, keepdims=True), (n, HD))


def widened(x):
    n = x.shape[0]
    chunks = x.shape[1] // HD
    i, j = iota((HD, 4 * HD), 0), iota((HD, 4 * HD), 1)
    e = mm(chunked(x), onehot((j & 255) == 2 * i + (j >> 8))).astype(BF)
    parts = [
        jnp.concatenate([e[g * n : (g + 1) * n, c * 256 : (c + 1) * 256] for g in range(chunks)], 1)
        for c in range(2)
    ]
    return jnp.concatenate(parts, 0)


def fetch_rows(flips, index_ref, n, width, w_at, w_ref, sems):
    me = index_ref[0]
    spots = []
    for flip in flips:
        for dc in range(2):
            peer = ((me >> 1) ^ flip) * 2 + ((me & 1) ^ dc)
            spots.append(pl.ds(pl.multiple_of(peer * (2 * width), 2 * width), 2 * width))
    steps = range(len(spots))
    return fetch([w_at.at[p] for p in spots], [w_ref.at[k] for k in steps], sems)


def project(widened_rows, w_ref, copies):
    total = 0.0
    for k, copy in enumerate(copies):
        both = widened_rows(k)
        copy.wait()
        total = total + mm(both, w_ref[k])
    return total


def wait_body(
    index_ref,
    mine_ref,
    across_ref,
    diagonal_ref,
    q_ref,
    pages_ref,
    tables_ref,
    lengths_ref,
    w_at,
    base_ref,
    cache_ref,
    w_ref,
    sems,
):
    _, n, width = mine_ref.shape
    copies = fetch_rows((0, 1), index_ref, n, width, w_at, w_ref, sems)
    attend_cached(q_ref, pages_ref, tables_ref, lengths_ref, cache_ref)
    rows = (
        lambda: widened(mine_ref[0]),
        lambda: widened(across_ref[...]),
        lambda: widened(mine_ref[1]),
        lambda: widened(diagonal_ref[...]),
    )
    base_ref[...] = project(lambda k: rows[k](), w_ref, copies)


def far_body(index_ref, mine_ref, other_ref, w_at, base_ref, w_ref, sems):
    _, n, width = mine_ref.shape
    copies = fetch_rows((3, 2), index_ref, n, width, w_at, w_ref, sems)
    base_ref[...] = project(
        lambda k: widened((mine_ref, other_ref)[k & 1][k >> 1]), w_ref, copies
    )


def finish_body(
    recv_ref, dest_ref, near_ref, far_ref, cos_ref, sin_ref, q_ref, cache_ref, att_ref, new_ref
):
    n = q_ref.shape[0]
    heads = q_ref.shape[1] // HD
    dest = dest_ref[...].astype(I32)
    dest = jnp.concatenate([dest, dest], 0)
    i, j = iota((2 * n, 1), 0), iota((1, 4 * n), 1)
    back = onehot((dest == (j >> 1)) & ((j & 1) == (i >> 5)))
    lora = mm(back, recv_ref[...])
    combined = near_ref[...] + far_ref[...] + ADAPTER_SCALE * lora
    key = combined[:n]
    half = HD // 2
    turned = jnp.concatenate([key[:, half:], key[:, :half]], 1)
    key = key * cos_ref[...] + turned * sin_ref[...]
    new = jnp.concatenate([key, combined[n:]], 0).astype(BF)
    i, j = iota((2 * n, 2 * n), 0), iota((2 * n, 2 * n), 1)
    new_ref[...] = mm(onehot((i & 1) * n + (i >> 1) == j), new).astype(BF)
    key = new[:n].astype(F32)
    value = new[n:].astype(F32)
    for h in range(heads):
        rows = slice(h * n, (h + 1) * n)
        q = q_ref[:, h * HD : (h + 1) * HD].astype(F32)
        own = jnp.sum(q * key, 1, keepdims=True) * (1.0 / math.sqrt(HD))
        top = cache_ref[1, rows, :]
        high = jnp.maximum(top, own)
        old = jnp.exp(top - high)
        mine = jnp.exp(own - high)
        mixed = cache_ref[0, rows, :] * old + mine * value
        att_ref[:, h * HD : (h + 1) * HD] = (mixed / (cache_ref[2, rows, :] * old + mine)).astype(BF)


def shape(dims, dtype):
    return jax.ShapeDtypeStruct(dims, dtype)


def per_device(
    hidden, queries, w_kv, adapters_down, adapters_up, kv_pages, tenant_ids, owner_table, page_tables, lengths
):
    n = hidden.shape[0]
    width = hidden.shape[1]

    def swap(a, flip):
        return lax.ppermute(a, "tp", [(i, i ^ flip) for i in range(8)])

    def along_y(a):
        return [
            lax.ppermute(a, "tp", [(i, ((i // 2 + d) % 4) * 2 + i % 2) for i in range(8)])
            for d in (1, 2, 3)
        ]

    entries = owner_table.shape[0]
    send, dest = call(
        route_body,
        (shape((n * CHUNK, HD), BF), shape((n, HD), F32)),
        3,
        2 * 576 * 256 * 128,
        300000,
        scratch=(
            pltpu.VMEM((n, width), BF),
            pltpu.VMEM((1, n), I32),
            pltpu.VMEM((1, entries), I32),
            pltpu.SemaphoreType.DMA((3,)),
        ),
        limit=ALL,
        far=(0, 1, 2),
    )(hidden, tenant_ids.reshape(1, -1), owner_table.reshape(1, -1))
    send = send.reshape(n, CHUNK // 2, 2, HD)
    recv = lax.all_to_all(send, "pool", 0, 0, tiled=True).reshape(n * CHUNK, HD)

    _, tied = lax.optimization_barrier((send, hidden))
    beside, across, diagonal = swap(tied, 2), swap(tied, 1), swap(tied, 3)
    count = adapters_down.shape[0]
    first = call(
        early_body,
        shape((EARLY, *adapters_down.shape[1:]), BF),
        1,
        0,
        8000000,
        scratch=(pltpu.SemaphoreType.DMA((1,)),),
        limit=SOME,
        far=(0,),
    )(adapters_down)
    recv, first, beside, across, diagonal = lax.optimization_barrier(
        (recv, first, beside, across, diagonal)
    )

    part, slot, near = call(
        down_body,
        (shape((2 * n, HD), F32), shape((2 * n, HD), F32), shape((2, n, width), BF)),
        5,
        2 * 64 * 16 * 1024 * 128,
        4500000,
        scratch=(
            pltpu.VMEM((count - EARLY, *adapters_down.shape[1:]), BF),
            pltpu.VMEM((n * CHUNK, HD), F32),
            pltpu.SemaphoreType.DMA((1,)),
        ),
        limit=SOME,
        far=(4,),
    )(recv, first, hidden, beside, adapters_down)
    part = part + swap(part, 1)
    sums = along_y(part)
    _, tied = lax.optimization_barrier((part, near))
    far, far_across = swap(tied, 6), swap(tied, 7)
    back = call(up_body, shape((4 * n, HD), BF), 6, 2 * 128 * 2048 * 128, 600000)(
        part, *sums, slot, adapters_up.reshape(-1, HD)
    )
    sent = back.reshape(n, 2, 2, HD)
    result = lax.all_to_all(sent, "pool", 0, 0, tiled=True).reshape(4 * n, HD)
    _, queries, lengths = lax.optimization_barrier((back, queries, lengths))
    half = HD // 2
    frequency = 10000.0 ** (-jnp.arange(half, dtype=F32) * 2.0 / HD)
    angles = lengths.astype(F32)[:, None] * frequency
    cosine, sine = jnp.cos(angles), jnp.sin(angles)
    cosine = jnp.concatenate([cosine, cosine], 1)
    sine = jnp.concatenate([-sine, sine], 1)

    pages = kv_pages.reshape(-1, HD)
    me = lax.axis_index("tp").astype(I32).reshape(1)
    base, cache = call(
        wait_body,
        (shape((2 * n, HD), F32), shape((3, 8 * n, HD), F32)),
        9,
        4 * 64 * 8192 * 128 + 4 * 256 * 1024 * 128,
        16000000,
        scratch=(
            pltpu.VMEM((4, 2 * width, HD), BF),
            pltpu.SemaphoreType.DMA((4,)),
        ),
        limit=MOST,
        smem=(0,),
        far=(8,),
    )(
        me,
        near,
        across,
        diagonal,
        queries,
        pages,
        page_tables.T,
        lengths.reshape(1, -1),
        w_kv.reshape(-1, HD),
    )

    rest = call(
        far_body,
        shape((2 * n, HD), F32),
        4,
        0,
        1000,
        scratch=(pltpu.VMEM((4, 2 * width, HD), BF), pltpu.SemaphoreType.DMA((4,))),
        limit=MOST,
        smem=(0,),
        far=(3,),
    )(me, far, far_across, w_kv.reshape(-1, HD))

    attention, new_kv = call(
        finish_body, (shape((n, width), BF), shape((2 * n, HD), BF)), 8, 1000000, 1000000
    )(result, dest, base, rest, cosine, sine, queries, cache)
    return attention, new_kv.reshape(n, 2, HD)


def solution(mesh):
    in_specs = (
        P("pool", "tp"),
        P("pool", "tp"),
        P(None, None, "tp"),
        P("pool", "tp", None),
        P("pool", None, None, "tp"),
        P("pool", None, None, "tp"),
        P("pool"),
        P(),
        P("pool", None),
        P("pool"),
    )
    out_specs = (P("pool", "tp"), P("pool", None, "tp"))
    return jax.shard_map(
        per_device, mesh=mesh, in_specs=in_specs, out_specs=out_specs, check_vma=False
    )
```

```python
import math

import jax
import jax.numpy as jnp
from jax import lax
from jax.experimental import pallas as pl
from jax.experimental.pallas import tpu as pltpu
from jax.sharding import PartitionSpec as P

HD = 128
ADAPTER_SCALE = 0.5
BF = jnp.bfloat16
F32 = jnp.float32
I32 = jnp.int32
VMEM = pl.BlockSpec(memory_space=pltpu.VMEM)
SMEM = pl.BlockSpec(memory_space=pltpu.SMEM)
HBM = pl.BlockSpec(memory_space=pl.ANY)
ALL = 58
MOST = 52
SOME = 50
EARLY = 6
CHUNK = 18


def iota(shape, dim):
    return lax.broadcasted_iota(I32, shape, dim)


def mm(a, b):
    return jnp.dot(a, b, preferred_element_type=F32)


def mm_t(a, b):
    return lax.dot_general(a, b, (((1,), (1,)), ((), ())), preferred_element_type=F32)


def onehot(mask):
    return jnp.where(mask, 1.0, 0.0).astype(BF)


def column(row, n):
    return jnp.sum(jnp.where(iota((n, n), 0) == iota((n, n), 1), row, 0.0), 1, keepdims=True)


def chunked(x):
    return jnp.concatenate([x[:, i * HD : (i + 1) * HD] for i in range(x.shape[1] // HD)], 0)


def call(body, outs, n_in, flops=0, read=0, scratch=(), limit=16, smem=(), far=()):
    return pl.pallas_call(
        body,
        out_shape=outs,
        in_specs=[SMEM if i in smem else HBM if i in far else VMEM for i in range(n_in)],
        out_specs=jax.tree.map(lambda _: VMEM, outs),
        scratch_shapes=scratch,
        compiler_params=pltpu.CompilerParams(vmem_limit_bytes=limit << 20),
        cost_estimate=pl.CostEstimate(flops=flops, bytes_accessed=read, transcendentals=0),
    )


def fetch(sources, targets, sems):
    copies = [
        pltpu.make_async_copy(source, target, sems.at[i])
        for i, (source, target) in enumerate(zip(sources, targets))
    ]
    for copy in copies:
        copy.start()
    return copies


def route_body(
    hidden_at, tenants_at, table_at, send_ref, dest_ref, hidden_ref, tenants_ref, table_ref, sems
):
    copies = fetch(
        (tenants_at, table_at, hidden_at), (tenants_ref, table_ref, hidden_ref), sems
    )
    copies[0].wait()
    copies[1].wait()
    n = tenants_ref.shape[1]
    tenant = column(tenants_ref[...].astype(F32), n)
    entries = table_ref.shape[1]
    table = table_ref[...].astype(F32)
    lanes = iota((n, entries), 1).astype(F32)
    storage = jnp.sum(jnp.where(tenant == lanes, table, 0.0), 1, keepdims=True).astype(I32)
    owner = (storage >> 4).astype(F32)
    slot = (storage & 15).astype(F32)
    eye = iota((n, n), 0) == iota((n, n), 1)
    owner_row = jnp.sum(jnp.where(eye, owner, 0.0), 0, keepdims=True)
    same = (owner == owner_row) & (iota((n, n), 1) < iota((n, n), 0))
    rank = jnp.sum(jnp.where(same, 1.0, 0.0), 1, keepdims=True)
    dest = owner * 2.0 + rank
    dest_ref[...] = jnp.broadcast_to(dest, dest_ref.shape)
    wide = (iota((n, 8 * n), 1) & (n - 1)) == iota((n, 8 * n), 0)
    dest_wide = jnp.sum(jnp.where(wide, dest, 0.0), 0, keepdims=True).astype(I32)
    dest_row = dest_wide[:, :n]
    i = iota((CHUNK * n, 1), 0)
    chunk = (i * 3641) >> 16
    rest = i - CHUNK * chunk
    place, part = chunk * 2 + (rest & 1), rest >> 1
    where_from = iota((1, 8 * n), 1)
    pick = onehot((place == dest_wide) & (part == (where_from >> 5)))
    pick_slot = onehot((place == dest_row) & (part == 8))
    slots = jnp.broadcast_to(slot, (n, HD)).astype(BF)
    sent = mm(pick_slot, slots)
    copies[2].wait()
    send_ref[...] = (sent + mm(pick, chunked(hidden_ref[...]))).astype(BF)


def early_body(down_at, first_ref, sems):
    (copy,) = fetch([down_at.at[: first_ref.shape[0]]], [first_ref], sems)
    copy.wait()


def down_body(
    recv_ref, first_ref, near_ref, beside_ref, down_at, part_ref, slot_ref, pair_ref, down_ref, wide_ref, sems
):
    early = first_ref.shape[0]
    (copy,) = fetch([down_at.at[early:]], [down_ref], sems)
    pair_ref[0] = near_ref[...]
    pair_ref[1] = beside_ref[...]
    n = recv_ref.shape[0] // CHUNK
    m = 2 * n
    wide_ref[...] = recv_ref[...].astype(F32)
    rows = wide_ref[...].reshape(n, CHUNK, HD)
    x = [rows[:, 2 * c : 2 * c + 2, :].reshape(m, HD).astype(BF) for c in range(CHUNK // 2 - 1)]
    x = jnp.concatenate(x, 1)
    slot = rows[:, CHUNK - 2 :, :].reshape(m, HD)
    slot_ref[...] = slot
    total = jnp.zeros((m, HD), F32)
    for a in range(0, down_at.shape[0], 2):
        if a < early:
            two = first_ref[a], first_ref[a + 1]
        else:
            if a == early:
                copy.wait()
            two = down_ref[a - early], down_ref[a - early + 1]
        y = mm(x, jnp.concatenate(two, 1))
        total = total + jnp.where(slot == a, y[:, :HD], 0.0)
        total = total + jnp.where(slot == a + 1, y[:, HD:], 0.0)
    part_ref[...] = total


def up_body(p0_ref, p1_ref, p2_ref, p3_ref, slot_ref, up_ref, send_ref):
    m = slot_ref.shape[0]
    down = (p0_ref[...] + p1_ref[...]) + (p2_ref[...] + p3_ref[...])
    first = iota((m, HD), 1) < HD // 2
    both = jnp.concatenate([jnp.where(first, down, 0.0), jnp.where(first, 0.0, down)], 0)
    slot = jnp.concatenate([slot_ref[...]] * 2, 0)
    count = up_ref.shape[0] // HD
    picked = jnp.concatenate(
        [jnp.where(slot == a, both, 0.0).astype(BF) for a in range(count)], 1
    )
    lora = mm(picked, up_ref[...])
    i, j = iota((2 * m, 1), 0), iota((1, 2 * m), 1)
    order = onehot((i & 1) * m + (i >> 1) == j)
    send_ref[...] = mm(order, lora.astype(BF)).astype(BF)


def attend_cached(q_ref, pages_ref, tables_ref, lengths_ref, cache_ref):
    n = q_ref.shape[0]
    heads = q_ref.shape[1] // HD
    page = HD
    count = pages_ref.shape[0] // (2 * page)
    tokens = count * page
    eye = onehot(iota((n, n), 0) == iota((n, n), 1))
    tables = mm_t(eye, tables_ref[...].astype(F32).astype(BF)).astype(I32)
    length = column(lengths_ref[...].astype(F32), n).astype(I32)
    at = iota((n, tokens), 1)
    page_id, place = at >> 7, at & (page - 1)
    counts = jnp.zeros((n, tokens), F32)
    for j in range(tables_ref.shape[0]):
        hit = (tables[:, j : j + 1] == page_id) & (place < length - j * page)
        counts = counts + jnp.where(hit, 1.0, 0.0)
    i, j = iota((2 * page, 2 * page), 0), iota((2 * page, 2 * page), 1)
    part = onehot((i & (page - 1)) * 2 + (i >> 7) == j)
    keys, values = [], []
    for p in range(count):
        both = mm(part, pages_ref[p * 2 * page : (p + 1) * 2 * page, :]).astype(BF)
        keys.append(both[:page])
        values.append(both[page:])
    keys = jnp.concatenate(keys, 0)
    values = jnp.concatenate(values, 0)
    absent = jnp.where(counts > 0.0, 0.0, -jnp.inf)
    for h in range(heads):
        scores = mm_t(q_ref[:, h * HD : (h + 1) * HD], keys) * (1.0 / math.sqrt(HD))
        scores = scores + absent
        top = jnp.max(scores, 1, keepdims=True)
        weights = jnp.exp(scores - top) * counts
        rows = slice(h * n, (h + 1) * n)
        cache_ref[0, rows, :] = mm(weights.astype(BF), values)
        cache_ref[1, rows, :] = jnp.broadcast_to(top, (n, HD))
        cache_ref[2, rows, :] = jnp.broadcast_to(jnp.sum(weights, 1, keepdims=True), (n, HD))


def widened(x):
    n = x.shape[0]
    chunks = x.shape[1] // HD
    i, j = iota((HD, 4 * HD), 0), iota((HD, 4 * HD), 1)
    e = mm(chunked(x), onehot((j & 255) == 2 * i + (j >> 8))).astype(BF)
    parts = [
        jnp.concatenate([e[g * n : (g + 1) * n, c * 256 : (c + 1) * 256] for g in range(chunks)], 1)
        for c in range(2)
    ]
    return jnp.concatenate(parts, 0)


def fetch_rows(flips, index_ref, n, width, w_at, w_ref, sems):
    me = index_ref[0]
    spots = []
    for flip in flips:
        for dc in range(2):
            peer = ((me >> 1) ^ flip) * 2 + ((me & 1) ^ dc)
            spots.append(pl.ds(pl.multiple_of(peer * (2 * width), 2 * width), 2 * width))
    steps = range(len(spots))
    return fetch([w_at.at[p] for p in spots], [w_ref.at[k] for k in steps], sems)


def project(widened_rows, w_ref, copies):
    total = 0.0
    for k, copy in enumerate(copies):
        both = widened_rows(k)
        copy.wait()
        total = total + mm(both, w_ref[k])
    return total


def near_body(index_ref, mine_ref, across_ref, diagonal_ref, w_at, base_ref, w_ref, sems):
    _, n, width = mine_ref.shape
    copies = fetch_rows((0, 1), index_ref, n, width, w_at, w_ref, sems)
    rows = (
        lambda: widened(mine_ref[0]),
        lambda: widened(across_ref[...]),
        lambda: widened(mine_ref[1]),
        lambda: widened(diagonal_ref[...]),
    )
    base_ref[...] = project(lambda k: rows[k](), w_ref, copies)


def far_body(index_ref, mine_ref, other_ref, w_at, base_ref, w_ref, sems):
    _, n, width = mine_ref.shape
    copies = fetch_rows((3, 2), index_ref, n, width, w_at, w_ref, sems)
    base_ref[...] = project(
        lambda k: widened((mine_ref, other_ref)[k & 1][k >> 1]), w_ref, copies
    )


def finish_body(
    recv_ref, dest_ref, near_ref, far_ref, cos_ref, sin_ref, q_ref, cache_ref, att_ref, new_ref
):
    n = q_ref.shape[0]
    heads = q_ref.shape[1] // HD
    dest = dest_ref[...].astype(I32)
    dest = jnp.concatenate([dest, dest], 0)
    i, j = iota((2 * n, 1), 0), iota((1, 4 * n), 1)
    back = onehot((dest == (j >> 1)) & ((j & 1) == (i >> 5)))
    lora = mm(back, recv_ref[...])
    combined = near_ref[...] + far_ref[...] + ADAPTER_SCALE * lora
    key = combined[:n]
    half = HD // 2
    turned = jnp.concatenate([key[:, half:], key[:, :half]], 1)
    key = key * cos_ref[...] + turned * sin_ref[...]
    new = jnp.concatenate([key, combined[n:]], 0).astype(BF)
    i, j = iota((2 * n, 2 * n), 0), iota((2 * n, 2 * n), 1)
    new_ref[...] = mm(onehot((i & 1) * n + (i >> 1) == j), new).astype(BF)
    key = new[:n].astype(F32)
    value = new[n:].astype(F32)
    for h in range(heads):
        rows = slice(h * n, (h + 1) * n)
        q = q_ref[:, h * HD : (h + 1) * HD].astype(F32)
        own = jnp.sum(q * key, 1, keepdims=True) * (1.0 / math.sqrt(HD))
        top = cache_ref[1, rows, :]
        high = jnp.maximum(top, own)
        old = jnp.exp(top - high)
        mine = jnp.exp(own - high)
        mixed = cache_ref[0, rows, :] * old + mine * value
        att_ref[:, h * HD : (h + 1) * HD] = (mixed / (cache_ref[2, rows, :] * old + mine)).astype(BF)


def shape(dims, dtype):
    return jax.ShapeDtypeStruct(dims, dtype)


def per_device(
    hidden, queries, w_kv, adapters_down, adapters_up, kv_pages, tenant_ids, owner_table, page_tables, lengths
):
    n = hidden.shape[0]
    width = hidden.shape[1]

    def swap(a, flip):
        return lax.ppermute(a, "tp", [(i, i ^ flip) for i in range(8)])

    def along_y(a):
        return [
            lax.ppermute(a, "tp", [(i, ((i // 2 + d) % 4) * 2 + i % 2) for i in range(8)])
            for d in (1, 2, 3)
        ]

    entries = owner_table.shape[0]
    send, dest = call(
        route_body,
        (shape((n * CHUNK, HD), BF), shape((n, HD), F32)),
        3,
        2 * 576 * 256 * 128,
        300000,
        scratch=(
            pltpu.VMEM((n, width), BF),
            pltpu.VMEM((1, n), I32),
            pltpu.VMEM((1, entries), I32),
            pltpu.SemaphoreType.DMA((3,)),
        ),
        limit=ALL,
        far=(0, 1, 2),
    )(hidden, tenant_ids.reshape(1, -1), owner_table.reshape(1, -1))
    send = send.reshape(n, CHUNK // 2, 2, HD)
    recv = lax.all_to_all(send, "pool", 0, 0, tiled=True).reshape(n * CHUNK, HD)

    _, tied = lax.optimization_barrier((send, hidden))
    beside, across, diagonal = swap(tied, 2), swap(tied, 1), swap(tied, 3)
    count = adapters_down.shape[0]
    first = call(
        early_body,
        shape((EARLY, *adapters_down.shape[1:]), BF),
        1,
        0,
        8000000,
        scratch=(pltpu.SemaphoreType.DMA((1,)),),
        limit=SOME,
        far=(0,),
    )(adapters_down)
    recv, first, beside, across, diagonal = lax.optimization_barrier(
        (recv, first, beside, across, diagonal)
    )

    part, slot, near = call(
        down_body,
        (shape((2 * n, HD), F32), shape((2 * n, HD), F32), shape((2, n, width), BF)),
        5,
        2 * 64 * 16 * 1024 * 128,
        4500000,
        scratch=(
            pltpu.VMEM((count - EARLY, *adapters_down.shape[1:]), BF),
            pltpu.VMEM((n * CHUNK, HD), F32),
            pltpu.SemaphoreType.DMA((1,)),
        ),
        limit=SOME,
        far=(4,),
    )(recv, first, hidden, beside, adapters_down)
    part = part + swap(part, 1)
    sums = along_y(part)
    _, tied = lax.optimization_barrier((part, near))
    far = swap(tied, 6)
    back = call(up_body, shape((4 * n, HD), BF), 6, 2 * 128 * 2048 * 128, 600000)(
        part, *sums, slot, adapters_up.reshape(-1, HD)
    )
    sent = back.reshape(n, 2, 2, HD)
    result = lax.all_to_all(sent, "pool", 0, 0, tiled=True).reshape(4 * n, HD)
    _, queries, lengths, near = lax.optimization_barrier((back, queries, lengths, near))
    half = HD // 2
    frequency = 10000.0 ** (-jnp.arange(half, dtype=F32) * 2.0 / HD)
    angles = lengths.astype(F32)[:, None] * frequency
    cosine, sine = jnp.cos(angles), jnp.sin(angles)
    cosine = jnp.concatenate([cosine, cosine], 1)
    sine = jnp.concatenate([-sine, sine], 1)

    pages = kv_pages.reshape(-1, HD)
    me = lax.axis_index("tp").astype(I32).reshape(1)
    cache = call(
        attend_cached,
        shape((3, 8 * n, HD), F32),
        4,
        4 * 256 * 1024 * 128,
        12000000,
        limit=MOST,
    )(queries, pages, page_tables.T, lengths.reshape(1, -1))
    cache, far = lax.optimization_barrier((cache, far))
    far_across = swap(far, 1)
    base = call(
        near_body,
        shape((2 * n, HD), F32),
        5,
        2 * 64 * 8192 * 128,
        4000000,
        scratch=(pltpu.VMEM((4, 2 * width, HD), BF), pltpu.SemaphoreType.DMA((4,))),
        limit=MOST,
        smem=(0,),
        far=(4,),
    )(me, near, across, diagonal, w_kv.reshape(-1, HD))

    rest = call(
        far_body,
        shape((2 * n, HD), F32),
        4,
        0,
        1000,
        scratch=(pltpu.VMEM((4, 2 * width, HD), BF), pltpu.SemaphoreType.DMA((4,))),
        limit=MOST,
        smem=(0,),
        far=(3,),
    )(me, far, far_across, w_kv.reshape(-1, HD))

    attention, new_kv = call(
        finish_body, (shape((n, width), BF), shape((2 * n, HD), BF)), 8, 1000000, 1000000
    )(result, dest, base, rest, cosine, sine, queries, cache)
    return attention, new_kv.reshape(n, 2, HD)


def solution(mesh):
    in_specs = (
        P("pool", "tp"),
        P("pool", "tp"),
        P(None, None, "tp"),
        P("pool", "tp", None),
        P("pool", None, None, "tp"),
        P("pool", None, None, "tp"),
        P("pool"),
        P(),
        P("pool", None),
        P("pool"),
    )
    out_specs = (P("pool", "tp"), P("pool", None, "tp"))
    return jax.shard_map(
        per_device, mesh=mesh, in_specs=in_specs, out_specs=out_specs, check_vma=False
    )
```

```python
import math

import jax
import jax.numpy as jnp
from jax import lax
from jax.experimental import pallas as pl
from jax.experimental.pallas import tpu as pltpu
from jax.sharding import PartitionSpec as P

HD = 128
ADAPTER_SCALE = 0.5
BF = jnp.bfloat16
F32 = jnp.float32
I32 = jnp.int32
VMEM = pl.BlockSpec(memory_space=pltpu.VMEM)
SMEM = pl.BlockSpec(memory_space=pltpu.SMEM)
HBM = pl.BlockSpec(memory_space=pl.ANY)
ALL = 58
MOST = 52
SOME = 50
EARLY = 6
CHUNK = 18


def iota(shape, dim):
    return lax.broadcasted_iota(I32, shape, dim)


def mm(a, b):
    return jnp.dot(a, b, preferred_element_type=F32)


def mm_t(a, b):
    return lax.dot_general(a, b, (((1,), (1,)), ((), ())), preferred_element_type=F32)


def onehot(mask):
    return jnp.where(mask, 1.0, 0.0).astype(BF)


def column(row, n):
    return jnp.sum(jnp.where(iota((n, n), 0) == iota((n, n), 1), row, 0.0), 1, keepdims=True)


def chunked(x):
    return jnp.concatenate([x[:, i * HD : (i + 1) * HD] for i in range(x.shape[1] // HD)], 0)


def call(body, outs, n_in, flops=0, read=0, scratch=(), limit=16, smem=(), far=()):
    return pl.pallas_call(
        body,
        out_shape=outs,
        in_specs=[SMEM if i in smem else HBM if i in far else VMEM for i in range(n_in)],
        out_specs=jax.tree.map(lambda _: VMEM, outs),
        scratch_shapes=scratch,
        compiler_params=pltpu.CompilerParams(vmem_limit_bytes=limit << 20),
        cost_estimate=pl.CostEstimate(flops=flops, bytes_accessed=read, transcendentals=0),
    )


def fetch(sources, targets, sems):
    copies = [
        pltpu.make_async_copy(source, target, sems.at[i])
        for i, (source, target) in enumerate(zip(sources, targets))
    ]
    for copy in copies:
        copy.start()
    return copies


def route_body(
    hidden_at, tenants_at, table_at, send_ref, dest_ref, hidden_ref, tenants_ref, table_ref, sems
):
    copies = fetch(
        (tenants_at, table_at, hidden_at), (tenants_ref, table_ref, hidden_ref), sems
    )
    copies[0].wait()
    copies[1].wait()
    n = tenants_ref.shape[1]
    tenants = jnp.concatenate([tenants_ref[...]] * 8, 1)
    entries = table_ref.shape[1]
    table = jnp.broadcast_to(table_ref[...], (8, entries))
    digits = jnp.where(iota((8, entries), 0) == 0, table >> 4, table & 15).astype(F32).astype(BF)
    found = mm(digits, onehot(iota((entries, 8 * n), 0) == tenants))
    owner, slot = found[0:1, :], found[1:2, :n]
    eye = iota((n, n), 0) == iota((n, n), 1)
    owner_column = jnp.sum(jnp.where(eye, owner[:, :n], 0.0), 1, keepdims=True)
    earlier = iota((n, 8 * n), 0) < (iota((n, 8 * n), 1) & (n - 1))
    rank = jnp.sum(jnp.where((owner_column == owner) & earlier, 1.0, 0.0), 0, keepdims=True)
    dest_all = owner * 2.0 + rank
    dest_wide = dest_all.astype(I32)
    dest_row = dest_wide[:, :n]
    i = iota((CHUNK * n, 1), 0)
    chunk = (i * 3641) >> 16
    rest = i - CHUNK * chunk
    place, part = chunk * 2 + (rest & 1), rest >> 1
    where_from = iota((1, 8 * n), 1)
    pick = onehot((place == dest_wide) & (part == (where_from >> 5)))
    pick_slot = onehot((place == dest_row) & (part == 8))
    slots = jnp.sum(jnp.where(eye, slot, 0.0), 1, keepdims=True)
    sent = mm(pick_slot, jnp.broadcast_to(slots, (n, HD)).astype(BF))
    copies[2].wait()
    send_ref[...] = (sent + mm(pick, chunked(hidden_ref[...]))).astype(BF)
    dest = jnp.sum(jnp.where(eye, dest_all[:, :n], 0.0), 1, keepdims=True)
    dest_ref[...] = jnp.broadcast_to(dest, dest_ref.shape)


def early_body(down_at, first_ref, sems):
    (copy,) = fetch([down_at.at[: first_ref.shape[0]]], [first_ref], sems)
    copy.wait()


def down_body(
    recv_ref, first_ref, near_ref, beside_ref, down_at, part_ref, slot_ref, pair_ref, down_ref, wide_ref, sems
):
    early = first_ref.shape[0]
    (copy,) = fetch([down_at.at[early:]], [down_ref], sems)
    pair_ref[0] = near_ref[...]
    pair_ref[1] = beside_ref[...]
    n = recv_ref.shape[0] // CHUNK
    m = 2 * n
    wide_ref[...] = recv_ref[...].astype(F32)
    rows = wide_ref[...].reshape(n, CHUNK, HD)
    x = [rows[:, 2 * c : 2 * c + 2, :].reshape(m, HD).astype(BF) for c in range(CHUNK // 2 - 1)]
    x = jnp.concatenate(x, 1)
    slot = rows[:, CHUNK - 2 :, :].reshape(m, HD)
    slot_ref[...] = slot
    total = jnp.zeros((m, HD), F32)
    for a in range(0, down_at.shape[0], 2):
        if a < early:
            two = first_ref[a], first_ref[a + 1]
        else:
            if a == early:
                copy.wait()
            two = down_ref[a - early], down_ref[a - early + 1]
        y = mm(x, jnp.concatenate(two, 1))
        total = total + jnp.where(slot == a, y[:, :HD], 0.0)
        total = total + jnp.where(slot == a + 1, y[:, HD:], 0.0)
    part_ref[...] = total


def up_body(p0_ref, p1_ref, p2_ref, p3_ref, slot_ref, up_ref, send_ref):
    m = slot_ref.shape[0]
    down = (p0_ref[...] + p1_ref[...]) + (p2_ref[...] + p3_ref[...])
    first = iota((m, HD), 1) < HD // 2
    both = jnp.concatenate([jnp.where(first, down, 0.0), jnp.where(first, 0.0, down)], 0)
    slot = jnp.concatenate([slot_ref[...]] * 2, 0)
    count = up_ref.shape[0] // HD
    picked = jnp.concatenate(
        [jnp.where(slot == a, both, 0.0).astype(BF) for a in range(count)], 1
    )
    lora = mm(picked, up_ref[...])
    i, j = iota((2 * m, 1), 0), iota((1, 2 * m), 1)
    order = onehot((i & 1) * m + (i >> 1) == j)
    send_ref[...] = mm(order, lora.astype(BF)).astype(BF)


def attend_cached(
    index_ref, q_ref, pages_ref, tables_ref, lengths_ref, w_at, cache_ref, w_ref, sems
):
    copies = fetch_rows((0, 1), index_ref, *q_ref.shape, w_at, w_ref, sems)
    n = q_ref.shape[0]
    heads = q_ref.shape[1] // HD
    page = HD
    count = pages_ref.shape[0] // (2 * page)
    tokens = count * page
    eye = onehot(iota((n, n), 0) == iota((n, n), 1))
    tables = mm_t(eye, tables_ref[...].astype(F32).astype(BF)).astype(I32)
    length = column(lengths_ref[...].astype(F32), n).astype(I32)
    at = iota((n, tokens), 1)
    page_id, place = at >> 7, at & (page - 1)
    counts = jnp.zeros((n, tokens), F32)
    for j in range(tables_ref.shape[0]):
        hit = (tables[:, j : j + 1] == page_id) & (place < length - j * page)
        counts = counts + jnp.where(hit, 1.0, 0.0)
    i, j = iota((2 * page, 2 * page), 0), iota((2 * page, 2 * page), 1)
    part = onehot((i & (page - 1)) * 2 + (i >> 7) == j)
    keys, values = [], []
    for p in range(count):
        both = mm(part, pages_ref[p * 2 * page : (p + 1) * 2 * page, :]).astype(BF)
        keys.append(both[:page])
        values.append(both[page:])
    keys = jnp.concatenate(keys, 0)
    values = jnp.concatenate(values, 0)
    absent = jnp.where(counts > 0.0, 0.0, -jnp.inf)
    for h in range(heads):
        scores = mm_t(q_ref[:, h * HD : (h + 1) * HD], keys) * (1.0 / math.sqrt(HD))
        scores = scores + absent
        top = jnp.max(scores, 1, keepdims=True)
        weights = jnp.exp(scores - top) * counts
        rows = slice(h * n, (h + 1) * n)
        cache_ref[0, rows, :] = mm(weights.astype(BF), values)
        cache_ref[1, rows, :] = jnp.broadcast_to(top, (n, HD))
        cache_ref[2, rows, :] = jnp.broadcast_to(jnp.sum(weights, 1, keepdims=True), (n, HD))
    for copy in copies:
        copy.wait()


def widened(x):
    n = x.shape[0]
    chunks = x.shape[1] // HD
    i, j = iota((HD, 4 * HD), 0), iota((HD, 4 * HD), 1)
    e = mm(chunked(x), onehot((j & 255) == 2 * i + (j >> 8))).astype(BF)
    parts = [
        jnp.concatenate([e[g * n : (g + 1) * n, c * 256 : (c + 1) * 256] for g in range(chunks)], 1)
        for c in range(2)
    ]
    return jnp.concatenate(parts, 0)


def fetch_rows(flips, index_ref, n, width, w_at, w_ref, sems):
    me = index_ref[0]
    spots = []
    for flip in flips:
        for dc in range(2):
            peer = ((me >> 1) ^ flip) * 2 + ((me & 1) ^ dc)
            spots.append(pl.ds(pl.multiple_of(peer * (2 * width), 2 * width), 2 * width))
    steps = range(len(spots))
    return fetch([w_at.at[p] for p in spots], [w_ref.at[k] for k in steps], sems)


def project(widened_rows, w_ref, copies):
    total = 0.0
    for k, copy in enumerate(copies):
        both = widened_rows(k)
        copy.wait()
        total = total + mm(both, w_ref[k])
    return total


def near_body(mine_ref, across_ref, diagonal_ref, w_ref, base_ref):
    parts = mine_ref[0], across_ref[...], mine_ref[1], diagonal_ref[...]
    base_ref[...] = sum(mm(widened(x), w_ref[k]) for k, x in enumerate(parts))


def far_body(index_ref, mine_ref, other_ref, w_at, base_ref, w_ref, sems):
    _, n, width = mine_ref.shape
    copies = fetch_rows((3, 2), index_ref, n, width, w_at, w_ref, sems)
    base_ref[...] = project(
        lambda k: widened((mine_ref, other_ref)[k & 1][k >> 1]), w_ref, copies
    )


def finish_body(
    recv_ref, dest_ref, near_ref, far_ref, cos_ref, sin_ref, q_ref, cache_ref, att_ref, new_ref
):
    n = q_ref.shape[0]
    heads = q_ref.shape[1] // HD
    dest = dest_ref[...].astype(I32)
    dest = jnp.concatenate([dest, dest], 0)
    i, j = iota((2 * n, 1), 0), iota((1, 4 * n), 1)
    back = onehot((dest == (j >> 1)) & ((j & 1) == (i >> 5)))
    lora = mm(back, recv_ref[...])
    combined = near_ref[...] + far_ref[...] + ADAPTER_SCALE * lora
    key = combined[:n]
    half = HD // 2
    turned = jnp.concatenate([key[:, half:], key[:, :half]], 1)
    key = key * cos_ref[...] + turned * sin_ref[...]
    new = jnp.concatenate([key, combined[n:]], 0).astype(BF)
    i, j = iota((2 * n, 2 * n), 0), iota((2 * n, 2 * n), 1)
    new_ref[...] = mm(onehot((i & 1) * n + (i >> 1) == j), new).astype(BF)
    key = new[:n].astype(F32)
    value = new[n:].astype(F32)
    for h in range(heads):
        rows = slice(h * n, (h + 1) * n)
        q = q_ref[:, h * HD : (h + 1) * HD].astype(F32)
        own = jnp.sum(q * key, 1, keepdims=True) * (1.0 / math.sqrt(HD))
        top = cache_ref[1, rows, :]
        high = jnp.maximum(top, own)
        old = jnp.exp(top - high)
        mine = jnp.exp(own - high)
        mixed = cache_ref[0, rows, :] * old + mine * value
        att_ref[:, h * HD : (h + 1) * HD] = (mixed / (cache_ref[2, rows, :] * old + mine)).astype(BF)


def shape(dims, dtype):
    return jax.ShapeDtypeStruct(dims, dtype)


def per_device(
    hidden, queries, w_kv, adapters_down, adapters_up, kv_pages, tenant_ids, owner_table, page_tables, lengths
):
    n = hidden.shape[0]
    width = hidden.shape[1]

    def swap(a, flip):
        return lax.ppermute(a, "tp", [(i, i ^ flip) for i in range(8)])

    def along_y(a):
        return [
            lax.ppermute(a, "tp", [(i, ((i // 2 + d) % 4) * 2 + i % 2) for i in range(8)])
            for d in (1, 2, 3)
        ]

    entries = owner_table.shape[0]
    send, dest = call(
        route_body,
        (shape((n * CHUNK, HD), BF), shape((n, HD), F32)),
        3,
        2 * 576 * 256 * 128,
        300000,
        scratch=(
            pltpu.VMEM((n, width), BF),
            pltpu.VMEM((1, n), I32),
            pltpu.VMEM((1, entries), I32),
            pltpu.SemaphoreType.DMA((3,)),
        ),
        limit=ALL,
        far=(0, 1, 2),
    )(hidden, tenant_ids.reshape(1, -1), owner_table.reshape(1, -1))
    send = send.reshape(n, CHUNK // 2, 2, HD)
    recv = lax.all_to_all(send, "pool", 0, 0, tiled=True).reshape(n * CHUNK, HD)

    _, tied = lax.optimization_barrier((send, hidden))
    beside, across, diagonal = swap(tied, 2), swap(tied, 1), swap(tied, 3)
    count = adapters_down.shape[0]
    first = call(
        early_body,
        shape((EARLY, *adapters_down.shape[1:]), BF),
        1,
        0,
        8000000,
        scratch=(pltpu.SemaphoreType.DMA((1,)),),
        limit=SOME,
        far=(0,),
    )(adapters_down)
    recv, first, beside, across, diagonal = lax.optimization_barrier(
        (recv, first, beside, across, diagonal)
    )

    part, slot, near = call(
        down_body,
        (shape((2 * n, HD), F32), shape((2 * n, HD), F32), shape((2, n, width), BF)),
        5,
        2 * 64 * 16 * 1024 * 128,
        4500000,
        scratch=(
            pltpu.VMEM((count - EARLY, *adapters_down.shape[1:]), BF),
            pltpu.VMEM((n * CHUNK, HD), F32),
            pltpu.SemaphoreType.DMA((1,)),
        ),
        limit=SOME,
        far=(4,),
    )(recv, first, hidden, beside, adapters_down)
    part = part + swap(part, 1)
    sums = along_y(part)
    _, tied = lax.optimization_barrier((part, near))
    far = swap(tied, 6)
    back = call(up_body, shape((4 * n, HD), BF), 6, 2 * 128 * 2048 * 128, 600000)(
        part, *sums, slot, adapters_up.reshape(-1, HD)
    )
    sent = back.reshape(n, 2, 2, HD)
    result = lax.all_to_all(sent, "pool", 0, 0, tiled=True).reshape(4 * n, HD)
    _, queries, lengths, near = lax.optimization_barrier((back, queries, lengths, near))
    half = HD // 2
    frequency = 10000.0 ** (-jnp.arange(half, dtype=F32) * 2.0 / HD)
    angles = lengths.astype(F32)[:, None] * frequency
    cosine, sine = jnp.cos(angles), jnp.sin(angles)
    cosine = jnp.concatenate([cosine, cosine], 1)
    sine = jnp.concatenate([-sine, sine], 1)

    pages = kv_pages.reshape(-1, HD)
    me = lax.axis_index("tp").astype(I32).reshape(1)
    cache, w_near = call(
        attend_cached,
        (shape((3, 8 * n, HD), F32), shape((4, 2 * width, HD), BF)),
        6,
        4 * 256 * 1024 * 128,
        12000000,
        scratch=(pltpu.SemaphoreType.DMA((4,)),),
        limit=SOME,
        smem=(0,),
        far=(5,),
    )(me, queries, pages, page_tables.T, lengths.reshape(1, -1), w_kv.reshape(-1, HD))
    cache, far = lax.optimization_barrier((cache, far))
    far_across = swap(far, 1)
    base = call(near_body, shape((2 * n, HD), F32), 4, 2 * 64 * 8192 * 128, 4000000, limit=SOME)(
        near, across, diagonal, w_near
    )

    rest = call(
        far_body,
        shape((2 * n, HD), F32),
        4,
        0,
        1000,
        scratch=(pltpu.VMEM((4, 2 * width, HD), BF), pltpu.SemaphoreType.DMA((4,))),
        limit=MOST,
        smem=(0,),
        far=(3,),
    )(me, far, far_across, w_kv.reshape(-1, HD))

    attention, new_kv = call(
        finish_body, (shape((n, width), BF), shape((2 * n, HD), BF)), 8, 1000000, 1000000
    )(result, dest, base, rest, cosine, sine, queries, cache)
    return attention, new_kv.reshape(n, 2, HD)


def solution(mesh):
    in_specs = (
        P("pool", "tp"),
        P("pool", "tp"),
        P(None, None, "tp"),
        P("pool", "tp", None),
        P("pool", None, None, "tp"),
        P("pool", None, None, "tp"),
        P("pool"),
        P(),
        P("pool", None),
        P("pool"),
    )
    out_specs = (P("pool", "tp"), P("pool", None, "tp"))
    return jax.shard_map(
        per_device, mesh=mesh, in_specs=in_specs, out_specs=out_specs, check_vma=False
    )
```

```python
import math

import jax
import jax.numpy as jnp
from jax import lax
from jax.experimental import pallas as pl
from jax.experimental.pallas import tpu as pltpu
from jax.sharding import PartitionSpec as P

HD = 128
ADAPTER_SCALE = 0.5
BF = jnp.bfloat16
F32 = jnp.float32
I32 = jnp.int32
VMEM = pl.BlockSpec(memory_space=pltpu.VMEM)
SMEM = pl.BlockSpec(memory_space=pltpu.SMEM)
HBM = pl.BlockSpec(memory_space=pl.ANY)
ALL = 58
MOST = 52
SOME = 50
EARLY = 6
CHUNK = 18


def iota(shape, dim):
    return lax.broadcasted_iota(I32, shape, dim)


def mm(a, b):
    return jnp.dot(a, b, preferred_element_type=F32)


def mm_t(a, b):
    return lax.dot_general(a, b, (((1,), (1,)), ((), ())), preferred_element_type=F32)


def onehot(mask):
    return jnp.where(mask, 1.0, 0.0).astype(BF)


def column(row, n):
    return jnp.sum(jnp.where(iota((n, n), 0) == iota((n, n), 1), row, 0.0), 1, keepdims=True)


def chunked(x):
    return jnp.concatenate([x[:, i * HD : (i + 1) * HD] for i in range(x.shape[1] // HD)], 0)


def call(body, outs, n_in, flops=0, read=0, scratch=(), limit=16, smem=(), far=()):
    return pl.pallas_call(
        body,
        out_shape=outs,
        in_specs=[SMEM if i in smem else HBM if i in far else VMEM for i in range(n_in)],
        out_specs=jax.tree.map(lambda _: VMEM, outs),
        scratch_shapes=scratch,
        compiler_params=pltpu.CompilerParams(vmem_limit_bytes=limit << 20),
        cost_estimate=pl.CostEstimate(flops=flops, bytes_accessed=read, transcendentals=0),
    )


def fetch(sources, targets, sems):
    copies = [
        pltpu.make_async_copy(source, target, sems.at[i])
        for i, (source, target) in enumerate(zip(sources, targets))
    ]
    for copy in copies:
        copy.start()
    return copies


def route_body(
    hidden_at, tenants_at, table_at, send_ref, dest_ref, hidden_ref, tenants_ref, table_ref, sems
):
    copies = fetch(
        (tenants_at, table_at, hidden_at), (tenants_ref, table_ref, hidden_ref), sems
    )
    copies[0].wait()
    copies[1].wait()
    n = tenants_ref.shape[1]
    tenants = jnp.concatenate([tenants_ref[...]] * 8, 1)
    entries = table_ref.shape[1]
    table = jnp.broadcast_to(table_ref[...], (8, entries))
    digits = jnp.where(iota((8, entries), 0) == 0, table >> 4, table & 15).astype(F32).astype(BF)
    found = mm(digits, onehot(iota((entries, 8 * n), 0) == tenants))
    owner, slot = found[0:1, :], found[1:2, :n]
    eye = iota((n, n), 0) == iota((n, n), 1)
    owner_column = jnp.sum(jnp.where(eye, owner[:, :n], 0.0), 1, keepdims=True)
    earlier = iota((n, 8 * n), 0) < (iota((n, 8 * n), 1) & (n - 1))
    rank = jnp.sum(jnp.where((owner_column == owner) & earlier, 1.0, 0.0), 0, keepdims=True)
    dest_all = owner * 2.0 + rank
    dest_wide = dest_all.astype(I32)
    dest_row = dest_wide[:, :n]
    i = iota((CHUNK * n, 1), 0)
    chunk = (i * 3641) >> 16
    rest = i - CHUNK * chunk
    place, part = chunk * 2 + (rest & 1), rest >> 1
    where_from = iota((1, 8 * n), 1)
    pick = onehot((place == dest_wide) & (part == (where_from >> 5)))
    pick_slot = onehot((place == dest_row) & (part == 8))
    slots = jnp.sum(jnp.where(eye, slot, 0.0), 1, keepdims=True)
    sent = mm(pick_slot, jnp.broadcast_to(slots, (n, HD)).astype(BF))
    copies[2].wait()
    send_ref[...] = (sent + mm(pick, chunked(hidden_ref[...]))).astype(BF)
    dest = jnp.sum(jnp.where(eye, dest_all[:, :n], 0.0), 1, keepdims=True)
    dest_ref[...] = jnp.broadcast_to(dest, dest_ref.shape)


def early_body(down_at, first_ref, sems):
    (copy,) = fetch([down_at.at[: first_ref.shape[0]]], [first_ref], sems)
    copy.wait()


def down_body(
    recv_ref, first_ref, near_ref, beside_ref, down_at, part_ref, slot_ref, pair_ref, down_ref, wide_ref, sems
):
    early = first_ref.shape[0]
    last = down_ref.shape[0] - 2
    copies = fetch(
        [down_at.at[early : early + last], down_at.at[early + last :]],
        [down_ref.at[:last], down_ref.at[last:]],
        sems,
    )
    pair_ref[0] = near_ref[...]
    pair_ref[1] = beside_ref[...]
    n = recv_ref.shape[0] // CHUNK
    m = 2 * n
    wide_ref[...] = recv_ref[...].astype(F32)
    rows = wide_ref[...].reshape(n, CHUNK, HD)
    x = [rows[:, 2 * c : 2 * c + 2, :].reshape(m, HD).astype(BF) for c in range(CHUNK // 2 - 1)]
    x = jnp.concatenate(x, 1)
    slot = rows[:, CHUNK - 2 :, :].reshape(m, HD)
    slot_ref[...] = slot
    total = jnp.zeros((m, HD), F32)
    for a in range(0, down_at.shape[0], 2):
        if a < early:
            two = first_ref[a], first_ref[a + 1]
        else:
            if a == early:
                copies[0].wait()
            if a == early + last:
                copies[1].wait()
            two = down_ref[a - early], down_ref[a - early + 1]
        y = mm(x, jnp.concatenate(two, 1))
        total = total + jnp.where(slot == a, y[:, :HD], 0.0)
        total = total + jnp.where(slot == a + 1, y[:, HD:], 0.0)
    part_ref[...] = total


def up_body(p0_ref, p1_ref, p2_ref, p3_ref, slot_ref, up_ref, send_ref):
    m = slot_ref.shape[0]
    down = (p0_ref[...] + p1_ref[...]) + (p2_ref[...] + p3_ref[...])
    first = iota((m, HD), 1) < HD // 2
    both = jnp.concatenate([jnp.where(first, down, 0.0), jnp.where(first, 0.0, down)], 0)
    slot = jnp.concatenate([slot_ref[...]] * 2, 0)
    count = up_ref.shape[0] // HD
    picked = jnp.concatenate(
        [jnp.where(slot == a, both, 0.0).astype(BF) for a in range(count)], 1
    )
    lora = mm(picked, up_ref[...])
    i, j = iota((2 * m, 1), 0), iota((1, 2 * m), 1)
    order = onehot((i & 1) * m + (i >> 1) == j)
    send_ref[...] = mm(order, lora.astype(BF)).astype(BF)


def attend_cached(
    index_ref, q_ref, pages_ref, tables_ref, lengths_ref, w_at, cache_ref, w_ref, sems
):
    copies = fetch_rows((0, 1), index_ref, *q_ref.shape, w_at, w_ref, sems)
    n = q_ref.shape[0]
    heads = q_ref.shape[1] // HD
    page = HD
    count = pages_ref.shape[0] // (2 * page)
    tokens = count * page
    eye = onehot(iota((n, n), 0) == iota((n, n), 1))
    tables = mm_t(eye, tables_ref[...].astype(F32).astype(BF)).astype(I32)
    length = column(lengths_ref[...].astype(F32), n).astype(I32)
    at = iota((n, tokens), 1)
    page_id, place = at >> 7, at & (page - 1)
    counts = jnp.zeros((n, tokens), F32)
    for j in range(tables_ref.shape[0]):
        hit = (tables[:, j : j + 1] == page_id) & (place < length - j * page)
        counts = counts + jnp.where(hit, 1.0, 0.0)
    i, j = iota((2 * page, 2 * page), 0), iota((2 * page, 2 * page), 1)
    part = onehot((i & (page - 1)) * 2 + (i >> 7) == j)
    keys, values = [], []
    for p in range(count):
        both = mm(part, pages_ref[p * 2 * page : (p + 1) * 2 * page, :]).astype(BF)
        keys.append(both[:page])
        values.append(both[page:])
    keys = jnp.concatenate(keys, 0)
    values = jnp.concatenate(values, 0)
    absent = jnp.where(counts > 0.0, 0.0, -jnp.inf)
    for h in range(heads):
        scores = mm_t(q_ref[:, h * HD : (h + 1) * HD], keys) * (1.0 / math.sqrt(HD))
        scores = scores + absent
        top = jnp.max(scores, 1, keepdims=True)
        weights = jnp.exp(scores - top) * counts
        rows = slice(h * n, (h + 1) * n)
        cache_ref[0, rows, :] = mm(weights.astype(BF), values)
        cache_ref[1, rows, :] = jnp.broadcast_to(top, (n, HD))
        cache_ref[2, rows, :] = jnp.broadcast_to(jnp.sum(weights, 1, keepdims=True), (n, HD))
    for copy in copies:
        copy.wait()


def widened(x):
    n = x.shape[0]
    chunks = x.shape[1] // HD
    i, j = iota((HD, 4 * HD), 0), iota((HD, 4 * HD), 1)
    e = mm(chunked(x), onehot((j & 255) == 2 * i + (j >> 8))).astype(BF)
    parts = [
        jnp.concatenate([e[g * n : (g + 1) * n, c * 256 : (c + 1) * 256] for g in range(chunks)], 1)
        for c in range(2)
    ]
    return jnp.concatenate(parts, 0)


def fetch_rows(flips, index_ref, n, width, w_at, w_ref, sems):
    me = index_ref[0]
    spots = []
    for flip in flips:
        for dc in range(2):
            peer = ((me >> 1) ^ flip) * 2 + ((me & 1) ^ dc)
            spots.append(pl.ds(pl.multiple_of(peer * (2 * width), 2 * width), 2 * width))
    steps = range(len(spots))
    return fetch([w_at.at[p] for p in spots], [w_ref.at[k] for k in steps], sems)


def project(widened_rows, w_ref, copies):
    total = 0.0
    for k, copy in enumerate(copies):
        both = widened_rows(k)
        copy.wait()
        total = total + mm(both, w_ref[k])
    return total


def near_body(mine_ref, across_ref, diagonal_ref, w_ref, base_ref):
    parts = mine_ref[0], across_ref[...], mine_ref[1], diagonal_ref[...]
    base_ref[...] = sum(mm(widened(x), w_ref[k]) for k, x in enumerate(parts))


def far_body(
    index_ref, mine_ref, other_ref, near_ref, dest_ref, w_at, base_ref, back_ref, w_ref, sems
):
    _, n, width = mine_ref.shape
    copies = fetch_rows((3, 2), index_ref, n, width, w_at, w_ref, sems)
    dest = dest_ref[...].astype(I32)
    dest = jnp.concatenate([dest, dest], 0)
    i, j = iota((2 * n, 1), 0), iota((1, 4 * n), 1)
    back_ref[...] = onehot((dest == (j >> 1)) & ((j & 1) == (i >> 5)))
    base_ref[...] = near_ref[...] + project(
        lambda k: widened((mine_ref, other_ref)[k & 1][k >> 1]), w_ref, copies
    )


def finish_body(
    recv_ref, back_ref, base_ref, cos_ref, sin_ref, q_ref, cache_ref, att_ref, new_ref
):
    n = q_ref.shape[0]
    heads = q_ref.shape[1] // HD
    lora = mm(back_ref[...], recv_ref[...])
    combined = base_ref[...] + ADAPTER_SCALE * lora
    key = combined[:n]
    half = HD // 2
    turned = jnp.concatenate([key[:, half:], key[:, :half]], 1)
    key = key * cos_ref[...] + turned * sin_ref[...]
    new = jnp.concatenate([key, combined[n:]], 0).astype(BF)
    i, j = iota((2 * n, 2 * n), 0), iota((2 * n, 2 * n), 1)
    new_ref[...] = mm(onehot((i & 1) * n + (i >> 1) == j), new).astype(BF)
    key = new[:n].astype(F32)
    value = new[n:].astype(F32)
    for h in range(heads):
        rows = slice(h * n, (h + 1) * n)
        q = q_ref[:, h * HD : (h + 1) * HD].astype(F32)
        own = jnp.sum(q * key, 1, keepdims=True) * (1.0 / math.sqrt(HD))
        top = cache_ref[1, rows, :]
        high = jnp.maximum(top, own)
        old = jnp.exp(top - high)
        mine = jnp.exp(own - high)
        mixed = cache_ref[0, rows, :] * old + mine * value
        att_ref[:, h * HD : (h + 1) * HD] = (mixed / (cache_ref[2, rows, :] * old + mine)).astype(BF)


def shape(dims, dtype):
    return jax.ShapeDtypeStruct(dims, dtype)


def per_device(
    hidden, queries, w_kv, adapters_down, adapters_up, kv_pages, tenant_ids, owner_table, page_tables, lengths
):
    n = hidden.shape[0]
    width = hidden.shape[1]

    def swap(a, flip):
        return lax.ppermute(a, "tp", [(i, i ^ flip) for i in range(8)])

    def along_y(a):
        return [
            lax.ppermute(a, "tp", [(i, ((i // 2 + d) % 4) * 2 + i % 2) for i in range(8)])
            for d in (1, 2, 3)
        ]

    entries = owner_table.shape[0]
    send, dest = call(
        route_body,
        (shape((n * CHUNK, HD), BF), shape((n, HD), F32)),
        3,
        2 * 576 * 256 * 128,
        300000,
        scratch=(
            pltpu.VMEM((n, width), BF),
            pltpu.VMEM((1, n), I32),
            pltpu.VMEM((1, entries), I32),
            pltpu.SemaphoreType.DMA((3,)),
        ),
        limit=ALL,
        far=(0, 1, 2),
    )(hidden, tenant_ids.reshape(1, -1), owner_table.reshape(1, -1))
    send = send.reshape(n, CHUNK // 2, 2, HD)
    recv = lax.all_to_all(send, "pool", 0, 0, tiled=True).reshape(n * CHUNK, HD)

    _, tied = lax.optimization_barrier((send, hidden))
    beside, across, diagonal = swap(tied, 2), swap(tied, 1), swap(tied, 3)
    count = adapters_down.shape[0]
    first = call(
        early_body,
        shape((EARLY, *adapters_down.shape[1:]), BF),
        1,
        0,
        8000000,
        scratch=(pltpu.SemaphoreType.DMA((1,)),),
        limit=SOME,
        far=(0,),
    )(adapters_down)
    recv, first, beside, across, diagonal = lax.optimization_barrier(
        (recv, first, beside, across, diagonal)
    )

    part, slot, near = call(
        down_body,
        (shape((2 * n, HD), F32), shape((2 * n, HD), F32), shape((2, n, width), BF)),
        5,
        2 * 64 * 16 * 1024 * 128,
        4500000,
        scratch=(
            pltpu.VMEM((count - EARLY, *adapters_down.shape[1:]), BF),
            pltpu.VMEM((n * CHUNK, HD), F32),
            pltpu.SemaphoreType.DMA((2,)),
        ),
        limit=SOME,
        far=(4,),
    )(recv, first, hidden, beside, adapters_down)
    part = part + swap(part, 1)
    sums = along_y(part)
    _, tied = lax.optimization_barrier((part, near))
    far = swap(tied, 6)
    back = call(up_body, shape((4 * n, HD), BF), 6, 2 * 128 * 2048 * 128, 600000)(
        part, *sums, slot, adapters_up.reshape(-1, HD)
    )
    sent = back.reshape(n, 2, 2, HD)
    result = lax.all_to_all(sent, "pool", 0, 0, tiled=True).reshape(4 * n, HD)
    _, queries, lengths, near = lax.optimization_barrier((back, queries, lengths, near))
    half = HD // 2
    frequency = 10000.0 ** (-jnp.arange(half, dtype=F32) * 2.0 / HD)
    angles = lengths.astype(F32)[:, None] * frequency
    cosine, sine = jnp.cos(angles), jnp.sin(angles)
    cosine = jnp.concatenate([cosine, cosine], 1)
    sine = jnp.concatenate([-sine, sine], 1)

    pages = kv_pages.reshape(-1, HD)
    me = lax.axis_index("tp").astype(I32).reshape(1)
    cache, w_near = call(
        attend_cached,
        (shape((3, 8 * n, HD), F32), shape((4, 2 * width, HD), BF)),
        6,
        4 * 256 * 1024 * 128,
        12000000,
        scratch=(pltpu.SemaphoreType.DMA((4,)),),
        limit=SOME,
        smem=(0,),
        far=(5,),
    )(me, queries, pages, page_tables.T, lengths.reshape(1, -1), w_kv.reshape(-1, HD))
    cache, far = lax.optimization_barrier((cache, far))
    far_across = swap(far, 1)
    base = call(near_body, shape((2 * n, HD), F32), 4, 2 * 64 * 8192 * 128, 4000000, limit=SOME)(
        near, across, diagonal, w_near
    )

    base, route = call(
        far_body,
        (shape((2 * n, HD), F32), shape((2 * n, 4 * n), BF)),
        6,
        0,
        1000,
        scratch=(pltpu.VMEM((4, 2 * width, HD), BF), pltpu.SemaphoreType.DMA((4,))),
        limit=MOST,
        smem=(0,),
        far=(5,),
    )(me, far, far_across, base, dest, w_kv.reshape(-1, HD))

    attention, new_kv = call(
        finish_body, (shape((n, width), BF), shape((2 * n, HD), BF)), 7, 1000000, 1000000
    )(result, route, base, cosine, sine, queries, cache)
    return attention, new_kv.reshape(n, 2, HD)


def solution(mesh):
    in_specs = (
        P("pool", "tp"),
        P("pool", "tp"),
        P(None, None, "tp"),
        P("pool", "tp", None),
        P("pool", None, None, "tp"),
        P("pool", None, None, "tp"),
        P("pool"),
        P(),
        P("pool", None),
        P("pool"),
    )
    out_specs = (P("pool", "tp"), P("pool", None, "tp"))
    return jax.shard_map(
        per_device, mesh=mesh, in_specs=in_specs, out_specs=out_specs, check_vma=False
    )
```

```python
import math

import jax
import jax.numpy as jnp
from jax import lax
from jax.experimental import pallas as pl
from jax.experimental.pallas import tpu as pltpu
from jax.sharding import PartitionSpec as P

HD = 128
ADAPTER_SCALE = 0.5
BF = jnp.bfloat16
F32 = jnp.float32
I32 = jnp.int32
VMEM = pl.BlockSpec(memory_space=pltpu.VMEM)
SMEM = pl.BlockSpec(memory_space=pltpu.SMEM)
HBM = pl.BlockSpec(memory_space=pl.ANY)
ALL = 58
MOST = 52
SOME = 50
EARLY = 6
CHUNK = 18


def iota(shape, dim):
    return lax.broadcasted_iota(I32, shape, dim)


def mm(a, b):
    return jnp.dot(a, b, preferred_element_type=F32)


def mm_t(a, b):
    return lax.dot_general(a, b, (((1,), (1,)), ((), ())), preferred_element_type=F32)


def onehot(mask):
    return jnp.where(mask, 1.0, 0.0).astype(BF)


def column(row, n):
    return jnp.sum(jnp.where(iota((n, n), 0) == iota((n, n), 1), row, 0.0), 1, keepdims=True)


def chunked(x):
    return jnp.concatenate([x[:, i * HD : (i + 1) * HD] for i in range(x.shape[1] // HD)], 0)


def call(body, outs, n_in, flops=0, read=0, scratch=(), limit=16, smem=(), far=()):
    return pl.pallas_call(
        body,
        out_shape=outs,
        in_specs=[SMEM if i in smem else HBM if i in far else VMEM for i in range(n_in)],
        out_specs=jax.tree.map(lambda _: VMEM, outs),
        scratch_shapes=scratch,
        compiler_params=pltpu.CompilerParams(vmem_limit_bytes=limit << 20),
        cost_estimate=pl.CostEstimate(flops=flops, bytes_accessed=read, transcendentals=0),
    )


def fetch(sources, targets, sems):
    copies = [
        pltpu.make_async_copy(source, target, sems.at[i])
        for i, (source, target) in enumerate(zip(sources, targets))
    ]
    for copy in copies:
        copy.start()
    return copies


def route_body(
    hidden_at, tenants_at, table_at, send_ref, dest_ref, hidden_ref, tenants_ref, table_ref, sems
):
    copies = fetch(
        (tenants_at, table_at, hidden_at), (tenants_ref, table_ref, hidden_ref), sems
    )
    copies[0].wait()
    copies[1].wait()
    n = tenants_ref.shape[1]
    tenants = jnp.concatenate([tenants_ref[...]] * 8, 1)
    entries = table_ref.shape[1]
    table = jnp.broadcast_to(table_ref[...], (8, entries))
    digits = jnp.where(iota((8, entries), 0) == 0, table >> 4, table & 15).astype(F32).astype(BF)
    found = mm(digits, onehot(iota((entries, 8 * n), 0) == tenants))
    owner, slot = found[0:1, :], found[1:2, :n]
    eye = iota((n, n), 0) == iota((n, n), 1)
    owner_column = jnp.sum(jnp.where(eye, owner[:, :n], 0.0), 1, keepdims=True)
    earlier = iota((n, 8 * n), 0) < (iota((n, 8 * n), 1) & (n - 1))
    rank = jnp.sum(jnp.where((owner_column == owner) & earlier, 1.0, 0.0), 0, keepdims=True)
    dest_all = owner * 2.0 + rank
    dest_wide = dest_all.astype(I32)
    dest_row = dest_wide[:, :n]
    i = iota((CHUNK * n, 1), 0)
    chunk = (i * 3641) >> 16
    rest = i - CHUNK * chunk
    place, part = chunk * 2 + (rest & 1), rest >> 1
    where_from = iota((1, 8 * n), 1)
    pick = onehot((place == dest_wide) & (part == (where_from >> 5)))
    pick_slot = onehot((place == dest_row) & (part == 8))
    slots = jnp.sum(jnp.where(eye, slot, 0.0), 1, keepdims=True)
    sent = mm(pick_slot, jnp.broadcast_to(slots, (n, HD)).astype(BF))
    copies[2].wait()
    send_ref[...] = (sent + mm(pick, chunked(hidden_ref[...]))).astype(BF)
    dest = jnp.sum(jnp.where(eye, dest_all[:, :n], 0.0), 1, keepdims=True)
    dest_ref[...] = jnp.broadcast_to(dest, dest_ref.shape)


def early_body(down_at, first_ref, sems):
    (copy,) = fetch([down_at.at[: first_ref.shape[0]]], [first_ref], sems)
    copy.wait()


def down_body(
    recv_ref, first_ref, near_ref, beside_ref, down_at, part_ref, slot_ref, pair_ref, down_ref, wide_ref, sems
):
    early = first_ref.shape[0]
    (copy,) = fetch([down_at.at[early:]], [down_ref], sems)
    pair_ref[0] = near_ref[...]
    pair_ref[1] = beside_ref[...]
    n = recv_ref.shape[0] // CHUNK
    m = 2 * n
    wide_ref[...] = recv_ref[...].astype(F32)
    rows = wide_ref[...].reshape(n, CHUNK, HD)
    x = [rows[:, 2 * c : 2 * c + 2, :].reshape(m, HD).astype(BF) for c in range(CHUNK // 2 - 1)]
    x = jnp.concatenate(x, 1)
    slot = rows[:, CHUNK - 2 :, :].reshape(m, HD)
    slot_ref[...] = slot
    total = jnp.zeros((m, HD), F32)
    for a in range(0, down_at.shape[0], 2):
        if a < early:
            two = first_ref[a], first_ref[a + 1]
        else:
            if a == early:
                copy.wait()
            two = down_ref[a - early], down_ref[a - early + 1]
        y = mm(x, jnp.concatenate(two, 1))
        total = total + jnp.where(slot == a, y[:, :HD], 0.0)
        total = total + jnp.where(slot == a + 1, y[:, HD:], 0.0)
    part_ref[...] = total


def up_body(p0_ref, p1_ref, p2_ref, p3_ref, slot_ref, up_ref, send_ref):
    m = slot_ref.shape[0]
    down = (p0_ref[...] + p1_ref[...]) + (p2_ref[...] + p3_ref[...])
    first = iota((m, HD), 1) < HD // 2
    both = jnp.concatenate([jnp.where(first, down, 0.0), jnp.where(first, 0.0, down)], 0)
    slot = jnp.concatenate([slot_ref[...]] * 2, 0)
    count = up_ref.shape[0] // HD
    picked = jnp.concatenate(
        [jnp.where(slot == a, both, 0.0).astype(BF) for a in range(count)], 1
    )
    lora = mm(picked, up_ref[...])
    i, j = iota((2 * m, 1), 0), iota((1, 2 * m), 1)
    order = onehot((i & 1) * m + (i >> 1) == j)
    send_ref[...] = mm(order, lora.astype(BF)).astype(BF)


def attend_cached(
    index_ref, q_ref, pages_ref, tables_ref, lengths_ref, w_at, cache_ref, w_ref, sems
):
    copies = fetch_rows((0, 1), index_ref, *q_ref.shape, w_at, w_ref, sems)
    n = q_ref.shape[0]
    heads = q_ref.shape[1] // HD
    page = HD
    count = pages_ref.shape[0] // (2 * page)
    tokens = count * page
    eye = onehot(iota((n, n), 0) == iota((n, n), 1))
    tables = mm_t(eye, tables_ref[...].astype(F32).astype(BF)).astype(I32)
    length = column(lengths_ref[...].astype(F32), n).astype(I32)
    at = iota((n, tokens), 1)
    page_id, place = at >> 7, at & (page - 1)
    counts = jnp.zeros((n, tokens), F32)
    for j in range(tables_ref.shape[0]):
        hit = (tables[:, j : j + 1] == page_id) & (place < length - j * page)
        counts = counts + jnp.where(hit, 1.0, 0.0)
    i, j = iota((2 * page, 2 * page), 0), iota((2 * page, 2 * page), 1)
    part = onehot((i & (page - 1)) * 2 + (i >> 7) == j)
    keys, values = [], []
    for p in range(count):
        both = mm(part, pages_ref[p * 2 * page : (p + 1) * 2 * page, :]).astype(BF)
        keys.append(both[:page])
        values.append(both[page:])
    keys = jnp.concatenate(keys, 0)
    values = jnp.concatenate(values, 0)
    absent = jnp.where(counts > 0.0, 0.0, -jnp.inf)
    for h in range(heads):
        scores = mm_t(q_ref[:, h * HD : (h + 1) * HD], keys) * (1.0 / math.sqrt(HD))
        scores = scores + absent
        top = jnp.max(scores, 1, keepdims=True)
        weights = jnp.exp(scores - top) * counts
        rows = slice(h * n, (h + 1) * n)
        cache_ref[0, rows, :] = mm(weights.astype(BF), values)
        cache_ref[1, rows, :] = jnp.broadcast_to(top, (n, HD))
        cache_ref[2, rows, :] = jnp.broadcast_to(jnp.sum(weights, 1, keepdims=True), (n, HD))
    for copy in copies:
        copy.wait()


def widened(x):
    n = x.shape[0]
    chunks = x.shape[1] // HD
    i, j = iota((HD, 4 * HD), 0), iota((HD, 4 * HD), 1)
    e = mm(chunked(x), onehot((j & 255) == 2 * i + (j >> 8))).astype(BF)
    parts = [
        jnp.concatenate([e[g * n : (g + 1) * n, c * 256 : (c + 1) * 256] for g in range(chunks)], 1)
        for c in range(2)
    ]
    return jnp.concatenate(parts, 0)


def fetch_rows(flips, index_ref, n, width, w_at, w_ref, sems):
    me = index_ref[0]
    spots = []
    for flip in flips:
        for dc in range(2):
            peer = ((me >> 1) ^ flip) * 2 + ((me & 1) ^ dc)
            spots.append(pl.ds(pl.multiple_of(peer * (2 * width), 2 * width), 2 * width))
    steps = range(len(spots))
    return fetch([w_at.at[p] for p in spots], [w_ref.at[k] for k in steps], sems)


def project(widened_rows, w_ref, copies):
    total = 0.0
    for k, copy in enumerate(copies):
        both = widened_rows(k)
        copy.wait()
        total = total + mm(both, w_ref[k])
    return total


def near_body(mine_ref, across_ref, diagonal_ref, w_ref, base_ref):
    parts = mine_ref[0], across_ref[...], mine_ref[1], diagonal_ref[...]
    base_ref[...] = sum(mm(widened(x), w_ref[k]) for k, x in enumerate(parts))


def far_body(index_ref, mine_ref, other_ref, w_at, base_ref, w_ref, sems):
    _, n, width = mine_ref.shape
    copies = fetch_rows((3, 2), index_ref, n, width, w_at, w_ref, sems)
    base_ref[...] = project(
        lambda k: widened((mine_ref, other_ref)[k & 1][k >> 1]), w_ref, copies
    )


def finish_body(
    recv_ref, dest_ref, near_ref, far_ref, cos_ref, sin_ref, q_ref, cache_ref, att_ref, new_ref
):
    n = q_ref.shape[0]
    heads = q_ref.shape[1] // HD
    dest = dest_ref[...].astype(I32)
    dest = jnp.concatenate([dest, dest], 0)
    i, j = iota((2 * n, 1), 0), iota((1, 4 * n), 1)
    back = onehot((dest == (j >> 1)) & ((j & 1) == (i >> 5)))
    lora = mm(back, recv_ref[...])
    combined = near_ref[...] + far_ref[...] + ADAPTER_SCALE * lora
    key = combined[:n]
    half = HD // 2
    turned = jnp.concatenate([key[:, half:], key[:, :half]], 1)
    key = key * cos_ref[...] + turned * sin_ref[...]
    new = jnp.concatenate([key, combined[n:]], 0).astype(BF)
    i, j = iota((2 * n, 2 * n), 0), iota((2 * n, 2 * n), 1)
    new_ref[...] = mm(onehot((i & 1) * n + (i >> 1) == j), new).astype(BF)
    key = new[:n].astype(F32)
    value = new[n:].astype(F32)
    for h in range(heads):
        rows = slice(h * n, (h + 1) * n)
        q = q_ref[:, h * HD : (h + 1) * HD].astype(F32)
        own = jnp.sum(q * key, 1, keepdims=True) * (1.0 / math.sqrt(HD))
        top = cache_ref[1, rows, :]
        high = jnp.maximum(top, own)
        old = jnp.exp(top - high)
        mine = jnp.exp(own - high)
        mixed = cache_ref[0, rows, :] * old + mine * value
        att_ref[:, h * HD : (h + 1) * HD] = (mixed / (cache_ref[2, rows, :] * old + mine)).astype(BF)


def shape(dims, dtype):
    return jax.ShapeDtypeStruct(dims, dtype)


def per_device(
    hidden, queries, w_kv, adapters_down, adapters_up, kv_pages, tenant_ids, owner_table, page_tables, lengths
):
    n = hidden.shape[0]
    width = hidden.shape[1]

    def swap(a, flip):
        return lax.ppermute(a, "tp", [(i, i ^ flip) for i in range(8)])

    def along_y(a):
        return [
            lax.ppermute(a, "tp", [(i, ((i // 2 + d) % 4) * 2 + i % 2) for i in range(8)])
            for d in (1, 2, 3)
        ]

    entries = owner_table.shape[0]
    send, dest = call(
        route_body,
        (shape((n * CHUNK, HD), BF), shape((n, HD), F32)),
        3,
        2 * 576 * 256 * 128,
        300000,
        scratch=(
            pltpu.VMEM((n, width), BF),
            pltpu.VMEM((1, n), I32),
            pltpu.VMEM((1, entries), I32),
            pltpu.SemaphoreType.DMA((3,)),
        ),
        limit=ALL,
        far=(0, 1, 2),
    )(hidden, tenant_ids.reshape(1, -1), owner_table.reshape(1, -1))
    send = send.reshape(n, CHUNK // 2, 2, HD)
    recv = lax.all_to_all(send, "pool", 0, 0, tiled=True).reshape(n * CHUNK, HD)

    _, tied = lax.optimization_barrier((send, hidden))
    beside, across, diagonal = swap(tied, 2), swap(tied, 1), swap(tied, 3)
    count = adapters_down.shape[0]
    first = call(
        early_body,
        shape((EARLY, *adapters_down.shape[1:]), BF),
        1,
        0,
        8000000,
        scratch=(pltpu.SemaphoreType.DMA((1,)),),
        limit=SOME,
        far=(0,),
    )(adapters_down)
    recv, first, beside, across, diagonal = lax.optimization_barrier(
        (recv, first, beside, across, diagonal)
    )

    part, slot, near = call(
        down_body,
        (shape((2 * n, HD), F32), shape((2 * n, HD), F32), shape((2, n, width), BF)),
        5,
        2 * 64 * 16 * 1024 * 128,
        4500000,
        scratch=(
            pltpu.VMEM((count - EARLY, *adapters_down.shape[1:]), BF),
            pltpu.VMEM((n * CHUNK, HD), F32),
            pltpu.SemaphoreType.DMA((1,)),
        ),
        limit=SOME,
        far=(4,),
    )(recv, first, hidden, beside, adapters_down)
    crossed = swap(part, 1)
    far = swap(near, 6)
    part = part + crossed
    sums = along_y(part)
    back = call(up_body, shape((4 * n, HD), BF), 6, 2 * 128 * 2048 * 128, 600000)(
        part, *sums, slot, adapters_up.reshape(-1, HD)
    )
    sent = back.reshape(n, 2, 2, HD)
    result = lax.all_to_all(sent, "pool", 0, 0, tiled=True).reshape(4 * n, HD)
    _, queries, lengths, near = lax.optimization_barrier((back, queries, lengths, near))
    half = HD // 2
    frequency = 10000.0 ** (-jnp.arange(half, dtype=F32) * 2.0 / HD)
    angles = lengths.astype(F32)[:, None] * frequency
    cosine, sine = jnp.cos(angles), jnp.sin(angles)
    cosine = jnp.concatenate([cosine, cosine], 1)
    sine = jnp.concatenate([-sine, sine], 1)

    pages = kv_pages.reshape(-1, HD)
    me = lax.axis_index("tp").astype(I32).reshape(1)
    cache, w_near = call(
        attend_cached,
        (shape((3, 8 * n, HD), F32), shape((4, 2 * width, HD), BF)),
        6,
        4 * 256 * 1024 * 128,
        12000000,
        scratch=(pltpu.SemaphoreType.DMA((4,)),),
        limit=SOME,
        smem=(0,),
        far=(5,),
    )(me, queries, pages, page_tables.T, lengths.reshape(1, -1), w_kv.reshape(-1, HD))
    cache, far = lax.optimization_barrier((cache, far))
    far_across = swap(far, 1)
    base = call(near_body, shape((2 * n, HD), F32), 4, 2 * 64 * 8192 * 128, 4000000, limit=SOME)(
        near, across, diagonal, w_near
    )

    rest = call(
        far_body,
        shape((2 * n, HD), F32),
        4,
        0,
        1000,
        scratch=(pltpu.VMEM((4, 2 * width, HD), BF), pltpu.SemaphoreType.DMA((4,))),
        limit=MOST,
        smem=(0,),
        far=(3,),
    )(me, far, far_across, w_kv.reshape(-1, HD))

    attention, new_kv = call(
        finish_body, (shape((n, width), BF), shape((2 * n, HD), BF)), 8, 1000000, 1000000
    )(result, dest, base, rest, cosine, sine, queries, cache)
    return attention, new_kv.reshape(n, 2, HD)


def solution(mesh):
    in_specs = (
        P("pool", "tp"),
        P("pool", "tp"),
        P(None, None, "tp"),
        P("pool", "tp", None),
        P("pool", None, None, "tp"),
        P("pool", None, None, "tp"),
        P("pool"),
        P(),
        P("pool", None),
        P("pool"),
    )
    out_specs = (P("pool", "tp"), P("pool", None, "tp"))
    return jax.shard_map(
        per_device, mesh=mesh, in_specs=in_specs, out_specs=out_specs, check_vma=False
    )
```
